32 devices in a mesh: slab: 8 (over z, y), px: 2 (over x), py: 2 (over core).
Axes of the slice: x: 2, y: 2, z: 4, core: 2. Of those that a mesh axis runs over, the one named last changes fastest.
Arguments:
- source: float32 [32, 4, 256, 256], P('slab', None, 'px', 'py'), may hold values from -6 to 6
- phase: float32 [32, 256, 256], P('slab', 'px', 'py'), may hold values from 0.3 to 2.8
- attenuation: float32 [32, 256, 256], P('slab', 'px', 'py'), may hold values from 0.003125 to 0.08
- pml_level: int32 [256, 256], P('px', 'py'), may hold values from 0 to 3
- recv_values: float32 [2, 2, 4, 4096], P('px', 'py', None, 'slab'), may hold values from -8 to 8
- recv_slab: int32 [2, 2, 4096, 1], P('px', 'py', 'slab'), may hold values from 0 to 7; in each aligned block of 512 rows (0 to 511, 512 to 1023, ..., all dimensions but the last counted through in order) at most 64 rows name the same one
- recv_lateral: int32 [2, 2, 4096], P('px', 'py', 'slab'), may hold values from 0 to 16383
- recv_layer: int32 [2, 2, 4096], P('px', 'py', 'slab'), may hold values from 0 to 3
Outputs:
- correction: float32 [32, 4, 256, 256], P('slab', None, 'px', 'py')
The draws below stay inside these ranges and needn't reach their ends.
Inputs may be any that keep to these rules, and one draw needn't show every extreme that they name: `recv_slab`: among the rows of one device, at most 64 receivers name the same slab, a bound that some block reaches of them.
All inputs are finite; a program needn't handle non-finite values.
Results may differ from the reference program's by a relative error of at most 0.000034.
Values sent between devices are 32-bit elements; how exact they have to be, the bound alone decides.
A program may use at most 128 MiB of HBM per device.

```python
import math
import jax
import jax.numpy as jnp
import numpy as np
from jax import lax

CX = 128
CY = 128
CZ = 4
SHOTS = 2
RECV_DEV = 512
COMP = 4
CAP = 64
RECV = 4096
NX = 256
NY = 256
NZ = 32
N_SLAB = 8
N_PX = 2
N_PY = 2


def place_ends(drawn, rng, smallest, top_value):
    longest = drawn.shape.index(max(drawn.shape))
    spots = []
    for shift in (0, 1):
        where = [jax.random.randint(jax.random.fold_in(rng, axis), (), 0, length) for axis, length in enumerate(drawn.shape)]
        where[longest] = (where[longest] + shift) % drawn.shape[longest]
        spots.append(tuple(where))
    return drawn.at[spots[0]].set(smallest).at[spots[1]].set(top_value)


def block_scale(stream_key, shape, cuts, low, high):
    loudness = 1.0
    for axis_at, blocks in cuts:
        steps = jax.random.uniform(jax.random.fold_in(jax.random.fold_in(stream_key, 6), axis_at), (blocks,), jnp.float32, low / len(cuts), high / len(cuts))
        loudness = loudness * jnp.repeat(jnp.exp(steps), shape[axis_at] // blocks).reshape((-1,) + (1,) * (len(shape) - 1 - axis_at))
    return loudness


def routed_block(rng, own, number, rows, number_of, top, limit, skew):
    ranking = jax.random.permutation(rng, number_of)
    crowded, ordinary = load_shares(number_of, rows * top, limit, skew, True), load_shares(number_of, rows * top, limit, skew, False)
    places = jnp.arange(number_of)

    def named(sizes, rotation):
        used = int((sizes > 0).sum())
        fixed = max(1, used // 4)
        shifted = fixed + (places - fixed + rotation * (used - fixed)) % max(1, number_of - fixed)
        return jnp.zeros((number_of,), jnp.int32).at[ranking[jnp.where(places < fixed, places, shifted)]].set(jnp.asarray(sizes, jnp.int32))

    sizes = jnp.where(number % 4 == 0, named(crowded, number // 4), named(ordinary, number - number // 4 - 1))
    mixed = jax.random.permutation(jax.random.fold_in(own, 3), number_of)
    donor, sink = mixed[0:number_of // 2 * 2:2], mixed[1:number_of // 2 * 2:2]
    room = jnp.minimum(sizes[donor] - 1, limit - sizes[sink]) // 2
    room = jnp.where((donor == ranking[0]) | (sink == ranking[0]) | (sizes[sink] == 0), 0, jnp.maximum(room, 0))
    shifted = jax.random.randint(jax.random.fold_in(own, 4), (number_of // 2,), 0, 1 << 20) % (room + 1)
    sizes = sizes.at[donor].add(-shifted).at[sink].add(shifted)
    labels = jnp.searchsorted(jnp.cumsum(sizes), jnp.arange(rows * top), side="right").astype(jnp.int32)
    listing = labels.reshape(top, rows).T
    listing = listing[jax.random.permutation(jax.random.fold_in(own, 1), rows)]
    rotation = jax.random.randint(jax.random.fold_in(own, 2), (rows, 1), 0, top)
    return jnp.take_along_axis(listing, (jnp.arange(top)[None, :] + rotation) % top, axis=1)


def load_shares(number_of, total, bound, lean, full):
    portions = [(1 << 20) // math.isqrt(grade ** lean) + 1 for grade in range(1, number_of + 1)]
    largest = bound if full else min(bound, max(-(-total // number_of), total * portions[0] // sum(portions)))
    least = 1 if total - largest >= number_of - 1 else 0
    given, spare = [largest] + [least] * (number_of - 1), total - largest - least * (number_of - 1)
    while spare > 0:
        movable = [i for i in range(1, number_of) if given[i] < largest] or [i for i in range(1, number_of) if given[i] < bound]
        mass, left = sum([portions[i] for i in movable]), spare
        for i in movable:
            extra = min(bound - given[i], max(1, left * portions[i] // mass), spare)
            given[i] = given[i] + extra
            spare = spare - extra
    return np.array(given)


def noise(rng, shape, scale, limit, pieces=(), kind=jnp.bfloat16):
    array = jax.random.normal(rng, shape, jnp.float32) * scale
    if len(pieces) > 0:
        array = block_scale(rng, shape, pieces, -0.22, 0.18) * array
    return jnp.clip(array, min=-limit, max=limit).astype(kind)


def setup_inputs(seed: int = 0) -> dict:
    streams_of = jax.random.split(jax.random.key(seed), 9)
    source = noise(streams_of[0], (NZ, COMP, NX, NY), 1.0, 6.0, ((0, 8), (2, 2), (3, 2)), jnp.float32)
    phase = jnp.clip(0.3 + 2.5 * jax.random.uniform(streams_of[1], (NZ, NX, NY), jnp.float32) ** block_scale(streams_of[1], (NZ, NX, NY), ((0, 8), (1, 2), (2, 2)), -0.2, 0.2), 0.3, 2.8)
    attenuation = jnp.clip(jnp.exp(math.log(0.08) - 3.2425923 * jax.random.uniform(streams_of[2], (NZ, NX, NY), jnp.float32) ** block_scale(streams_of[2], (NZ, NX, NY), ((0, 8), (1, 2), (2, 2)), -0.2, 0.2)), 0.003125, 0.08)
    pml_level = place_ends(jax.random.randint(streams_of[3], (NX, NY), 0, 4), jax.random.fold_in(streams_of[3], 1), 0, 3).astype(jnp.int32)
    recv_values = noise(streams_of[4], (N_PX, N_PY, COMP, RECV), 2.0, 8.0, ((0, 2), (1, 2), (3, 8)), jnp.float32)
    recv_slab_keys = jax.random.split(jax.random.fold_in(streams_of[5], 1), N_PX * N_PY * RECV // RECV_DEV)
    recv_slab_turns = jax.random.permutation(jax.random.fold_in(streams_of[5], 3), N_PX * N_PY * RECV // RECV_DEV)
    recv_slab = jax.vmap(lambda own, number: routed_block(jax.random.fold_in(streams_of[5], 2), own, number, RECV_DEV, N_SLAB, 1, CAP, 2))(recv_slab_keys, recv_slab_turns).reshape((N_PX, N_PY, RECV, 1))
    recv_lateral = place_ends(jax.random.randint(streams_of[6], (N_PX, N_PY, RECV), 0, CX * CY), jax.random.fold_in(streams_of[6], 1), 0, (CX * CY) - 1).astype(jnp.int32)
    recv_layer = place_ends(jax.random.randint(streams_of[7], (N_PX, N_PY, RECV), 0, CZ), jax.random.fold_in(streams_of[7], 1), 0, CZ - 1).astype(jnp.int32)
    return dict(source=source, phase=phase, attenuation=attenuation, pml_level=pml_level, recv_values=recv_values, recv_slab=recv_slab, recv_lateral=recv_lateral, recv_layer=recv_layer)


def march(state, layer):
    real_part, imag_part = state
    rate_real, rate_imag, force_layer = layer
    new_real = rate_real * real_part - rate_imag * imag_part + force_layer[:, 0]
    new_imag = rate_real * imag_part + rate_imag * real_part + force_layer[:, 1]
    return (new_real, new_imag), jnp.stack([new_real, new_imag], axis=1)


def reference(source, phase, attenuation, pml_level, recv_values, recv_slab, recv_lateral, recv_layer):
    damping = attenuation + (0.5 / NZ) * pml_level.astype(jnp.float32)[None, :, :]
    amplitude = jnp.exp(-damping)
    real_mult = amplitude * jnp.cos(phase)
    imag_mult = amplitude * jnp.sin(phase)
    tile_x = jnp.arange(N_PX, dtype=jnp.int32)[:, None, None]
    tile_y = jnp.arange(N_PY, dtype=jnp.int32)[None, :, None]
    depth_index = recv_slab[..., 0] * CZ + recv_layer
    cross_x = jnp.broadcast_to(tile_x * CX + recv_lateral // CY, depth_index.shape)
    cross_y = jnp.broadcast_to(tile_y * CY + recv_lateral % CY, depth_index.shape)
    forcing = source
    for column in range(COMP):
        forcing = forcing.at[depth_index, column, cross_x, cross_y].add(recv_values[:, :, column, :])
    fields = forcing.reshape(NZ, SHOTS, 2, NX, NY)
    zeros = jnp.zeros((SHOTS, NX, NY), jnp.float32)
    final_down, downward = lax.scan(march, (zeros, zeros), (real_mult, imag_mult, fields))
    final_up, upward = lax.scan(march, (zeros, zeros), (real_mult, imag_mult, fields), reverse=True)
    combined = (downward + upward - fields).reshape(NZ, COMP, NX, NY)
    padded = jnp.pad(combined, ((0, 0), (0, 0), (1, 1), (1, 1)))
    neighbours = padded[:, :, 2:, 1:-1] + padded[:, :, :-2, 1:-1] + padded[:, :, 1:-1, 2:] + padded[:, :, 1:-1, :-2]
    return combined - 0.2 * (4.0 * combined - neighbours)
```

```python
import functools

import jax
import jax.numpy as jnp
from jax import lax
from jax.experimental import pallas as pl
from jax.experimental.pallas import tpu as pltpu
from jax.sharding import PartitionSpec as P

CHUNKS = 4
LANES = 128
CAP = 64
BF16 = jnp.bfloat16
F32 = jnp.float32


def thirds(value):
    high = value.astype(BF16)
    rest = value - high.astype(F32)
    mid = rest.astype(BF16)
    low = (rest - mid.astype(F32)).astype(BF16)
    return high, mid, low


def times(rate, state):
    return rate[0] * state[0] - rate[1] * state[1], rate[0] * state[1] + rate[1] * state[0]


def kernel(
    sizes,
    src_hbm, phase_hbm, att_hbm, pml_hbm, vals, rslab, rlat, rlay,
    out,
    force, phase, att, pml, rate_re, rate_im,
    data, spread, arrived, left, right,
    prod_send, prod_pair, fwd_send, pair,
    down_send, down_recv, up_send, up_recv,
    down_back, up_back, enter_down, enter_up,
    comb, row_send, row_recv, col_send, col_recv,
    in_sem, spread_s, spread_r, prod_s, prod_r, fwd_s, fwd_r,
    down_s, down_r, up_s, up_r, dback_s, dback_r, uback_s, uback_r,
    row_s, row_r, col_s, col_r,
):
    S, L, C, X, Y, K = sizes
    G = S // 2
    H = X // 2
    R = H // K
    shots = C // 2
    me = lax.axis_index("slab")
    px = lax.axis_index("px")
    py = lax.axis_index("py")
    g = lax.div(me, 2)
    y = lax.rem(me, 2)
    partner = {"slab": g * 2 + (1 - y)}
    other_x = {"px": 1 - px}
    other_y = {"py": 1 - py}

    def remote(src, dst, send, recv, where):
        return pltpu.make_async_remote_copy(
            src_ref=src, dst_ref=dst, send_sem=send, recv_sem=recv,
            device_id=where, device_id_type=pl.DeviceIdType.MESH,
        )

    barrier = pltpu.get_barrier_semaphore()
    peers = [lax.rem(me + step, S) for step in range(1, S)]
    for where in [{"slab": peer} for peer in peers] + [other_x, other_y]:
        pl.semaphore_signal(barrier, inc=1, device_id=where, device_id_type=pl.DeviceIdType.MESH)

    loads = [
        pltpu.make_async_copy(a, b, in_sem.at[i])
        for i, (a, b) in enumerate(
            ((phase_hbm, phase), (att_hbm, att), (pml_hbm, pml), (src_hbm, force))
        )
    ]
    for load in loads:
        load.start()

    rows = vals.shape[1]
    lane = lax.broadcasted_iota(jnp.int32, (rows, LANES), 1)
    slab_of = rslab[...]
    hot = jnp.where(lane == slab_of, 1.0, 0.0)
    earlier = jnp.where(
        lax.broadcasted_iota(jnp.int32, (rows, rows), 1)
        < lax.broadcasted_iota(jnp.int32, (rows, rows), 0),
        1.0, 0.0,
    ).astype(BF16)
    before = jnp.dot(earlier, hot.astype(BF16), preferred_element_type=F32)
    rank = jnp.sum(before * hot, axis=1, keepdims=True).astype(jnp.int32)
    slot = slab_of * LANES + rank
    place = jnp.where(
        lax.broadcasted_iota(jnp.int32, (rows, S * LANES), 1) == slot, 1.0, 0.0
    ).astype(BF16)
    lateral = rlat[...]
    data[...] = jnp.zeros_like(data)
    data[0:C, :] = vals[...]
    data[C : C + 1, :] = (rlay[...] * X + lax.div(lateral, Y)).astype(F32)
    data[C + 1 : C + 2, :] = lax.rem(lateral, Y).astype(F32)
    routed = sum(
        jnp.dot(part, place, preferred_element_type=F32) for part in thirds(data[...])
    )
    for s in range(S):
        spread[s] = routed[:, s * LANES : (s + 1) * LANES]

    pl.semaphore_wait(barrier, S + 1)
    arrived[me] = spread[me]
    spreads = []
    for peer in peers:
        copy = remote(
            spread.at[peer], arrived.at[me], spread_s.at[peer], spread_r.at[me], {"slab": peer}
        )
        copy.start()
        spreads.append(copy)

    for load in loads[:3]:
        load.wait()
    for l in range(L):
        damping = att[l] + (0.5 / (L * S)) * pml[...].astype(F32)
        amplitude = jnp.exp(-damping)
        rate_re[l] = amplitude * jnp.cos(phase[l])
        rate_im[l] = amplitude * jnp.sin(phase[l])

    def product(half):
        at = pl.ds(pl.multiple_of(half * H, H), H)
        total = (rate_re[0, at], rate_im[0, at])
        for l in range(1, L):
            total = times((rate_re[l, at], rate_im[l, at]), total)
        return total

    total = product(1 - y)
    prod_send[0] = total[0]
    prod_send[1] = total[1]
    send_prod = remote(prod_send, prod_pair.at[y], prod_s, prod_r, partner)
    send_prod.start()
    total = product(y)
    prod_pair[y, 0] = total[0]
    prod_pair[y, 1] = total[1]

    loads[3].wait()
    for peer in peers:
        remote(
            spread.at[peer], arrived.at[peer], spread_s.at[peer], spread_r.at[peer], {"slab": peer}
        ).wait_recv()
    slots = S * CAP
    got = jnp.concatenate(
        [arrived[2 * i] + pltpu.roll(arrived[2 * i + 1], CAP, 1) for i in range(S // 2)], axis=1
    )
    row_at = got[C : C + 1, :].astype(jnp.int32)
    col_at = got[C + 1 : C + 2, :].astype(jnp.int32)
    on_row = jnp.where(
        lax.broadcasted_iota(jnp.int32, (L * X, slots), 0) == row_at, 1.0, 0.0
    ).astype(BF16)
    on_col = lax.broadcasted_iota(jnp.int32, (Y, slots), 0) == col_at
    parts = thirds(got)
    for i in range(3):
        left[:, i * slots : (i + 1) * slots] = on_row
        part = parts[i].astype(F32)
        for c in range(C):
            right[c * Y : (c + 1) * Y, i * slots : (i + 1) * slots] = jnp.where(
                on_col, part[c : c + 1, :], 0.0
            ).astype(BF16)
    for l in range(L):
        added = lax.dot_general(
            left[l * X : (l + 1) * X, :], right[...], (((1,), (1,)), ((), ())),
            preferred_element_type=F32,
        )
        for c in range(C):
            force[l, c] += added[:, c * Y : (c + 1) * Y]

    def local(half, k, dst):
        at = pl.ds(pl.multiple_of(half * H + k * R, R), R)
        rates = [(rate_re[l, at], rate_im[l, at]) for l in range(L)]
        for s in range(shots):
            f = [(force[l, 2 * s, at], force[l, 2 * s + 1, at]) for l in range(L)]
            w = f[0]
            for l in range(1, L):
                re, im = times(rates[l], w)
                w = (re + f[l][0], im + f[l][1])
            v = f[L - 1]
            for l in range(L - 2, -1, -1):
                re, im = times(rates[l], v)
                v = (re + f[l][0], im + f[l][1])
            dst[2 * s] = w[0]
            dst[2 * s + 1] = w[1]
            dst[C + 2 * s] = v[0]
            dst[C + 2 * s + 1] = v[1]

    sends = []
    for k in range(K):
        local(1 - y, k, fwd_send.at[k])
        copy = remote(fwd_send.at[k], pair.at[y, k], fwd_s.at[k], fwd_r.at[k], partner)
        copy.start()
        sends.append(copy)
    for k in range(K):
        local(y, k, pair.at[y, k])

    @pl.when(g == 0)
    def _():
        down_recv[...] = jnp.zeros_like(down_recv)

    @pl.when(g == G - 1)
    def _():
        up_recv[...] = jnp.zeros_like(up_recv)

    def down_copy(k):
        return remote(down_send.at[k], down_recv.at[k], down_s.at[k], down_r.at[k], {"slab": me + 2})

    def up_copy(k):
        return remote(up_send.at[k], up_recv.at[k], up_s.at[k], up_r.at[k], {"slab": me - 2})

    def down_back_copy(k):
        return remote(down_back.at[k], enter_down.at[y, k], dback_s.at[k], dback_r.at[k], partner)

    def up_back_copy(k):
        return remote(up_back.at[k], enter_up.at[y, k], uback_s.at[k], uback_r.at[k], partner)

    def factors(k, member):
        at = pl.ds(pl.multiple_of(k * R, R), R)
        return prod_pair[member, 0, at], prod_pair[member, 1, at]

    def hop(k, first, second, base, incoming, outgoing, own, theirs, own_direct):
        near, far = factors(k, first), factors(k, second)
        for s in range(shots):
            i, j = 2 * s, 2 * s + 1
            e = (incoming[k, i], incoming[k, j])
            re, im = times(near, e)
            q = (re + pair[first, k, base + i], im + pair[first, k, base + j])
            re, im = times(far, q)
            outgoing[k, i] = re + pair[second, k, base + i]
            outgoing[k, j] = im + pair[second, k, base + j]
            for a in (0, 1):
                own[y, k, 2 * s + a] = jnp.where(own_direct, e[a], q[a])
                theirs[k, 2 * s + a] = jnp.where(own_direct, q[a], e[a])

    send_prod.wait_recv()
    for t in range(K + G - 1):
        if t < K:
            remote(
                fwd_send.at[t], pair.at[1 - y, t], fwd_s.at[t], fwd_r.at[t], partner
            ).wait_recv()
        kd = t - g
        ku = t - (G - 1 - g)

        @pl.when((kd >= 0) & (kd < K))
        def _():
            @pl.when(g > 0)
            def _():
                remote(
                    down_send.at[kd], down_recv.at[kd], down_s.at[kd], down_r.at[kd], {"slab": me - 2}
                ).wait_recv()

            hop(kd, 0, 1, 0, down_recv, down_send, enter_down, down_back, y == 0)

            @pl.when(g < G - 1)
            def _():
                down_copy(kd).start()

            down_back_copy(kd).start()

        @pl.when((ku >= 0) & (ku < K))
        def _():
            @pl.when(g < G - 1)
            def _():
                remote(
                    up_send.at[ku], up_recv.at[ku], up_s.at[ku], up_r.at[ku], {"slab": me + 2}
                ).wait_recv()

            hop(ku, 1, 0, C, up_recv, up_send, enter_up, up_back, y == 1)

            @pl.when(g > 0)
            def _():
                up_copy(ku).start()

            up_back_copy(ku).start()

    pad = comb.shape[2] // 2 - X // 2

    def full(half, k):
        row = half * H + k * R
        at = pl.ds(pl.multiple_of(row, R), R)
        to = pl.ds(pl.multiple_of(row + pad, 8), R)
        rates = [(rate_re[l, at], rate_im[l, at]) for l in range(L)]
        for s in range(shots):
            i, j = 2 * s, 2 * s + 1
            f = [(force[l, i, at], force[l, j, at]) for l in range(L)]
            w = (enter_down[half, k, i], enter_down[half, k, j])
            downs = []
            for l in range(L):
                re, im = times(rates[l], w)
                w = (re + f[l][0], im + f[l][1])
                downs.append(w)
            v = (enter_up[half, k, i], enter_up[half, k, j])
            for l in range(L - 1, -1, -1):
                re, im = times(rates[l], v)
                comb[l, i, to] = downs[l][0] + re
                comb[l, j, to] = downs[l][1] + im
                v = (re + f[l][0], im + f[l][1])

    for k in range(K):
        full(y, k)
    for k in range(K):
        remote(
            down_back.at[k], enter_down.at[1 - y, k], dback_s.at[k], dback_r.at[k], partner
        ).wait_recv()
        remote(
            up_back.at[k], enter_up.at[1 - y, k], uback_s.at[k], uback_r.at[k], partner
        ).wait_recv()
        full(1 - y, k)

    edge_lane = lax.broadcasted_iota(jnp.int32, (X, LANES), 1)

    def send_rows(row):
        for l in range(L):
            for c in range(C):
                row_send[l * C + c : l * C + c + 1, :] = comb[l, c, pad + row : pad + row + 1, :]

    def send_cols(col):
        held = jnp.zeros((X, LANES), F32)
        for l in range(L):
            for c in range(C):
                column = comb[l, c, pad : pad + X, col : col + 1]
                held = jnp.where(edge_lane == l * C + c, column, held)
        col_send[...] = held

    pl.when(px == 0)(lambda: send_rows(X - 1))
    pl.when(px == 1)(lambda: send_rows(0))
    rows_out = remote(row_send, row_recv, row_s, row_r, other_x)
    rows_out.start()
    pl.when(py == 0)(lambda: send_cols(Y - 1))
    pl.when(py == 1)(lambda: send_cols(0))
    cols_out = remote(col_send, col_recv, col_s, col_r, other_y)
    cols_out.start()

    full_lane = lax.broadcasted_iota(jnp.int32, (X, Y), 1)
    for l in range(L):
        for c in range(C):
            comb[l, c, pad - 1 : pad, :] = jnp.zeros((1, Y), F32)
            comb[l, c, pad + X : pad + X + 1, :] = jnp.zeros((1, Y), F32)
            here = comb[l, c, pad : pad + X, :]
            around = comb[l, c, pad - 1 : pad - 1 + X, :] + comb[l, c, pad + 1 : pad + 1 + X, :]
            around += jnp.where(full_lane == 0, 0.0, pltpu.roll(here, 1, 1))
            around += jnp.where(full_lane == Y - 1, 0.0, pltpu.roll(here, Y - 1, 1))
            out[l, c] = here - 0.2 * (4.0 * here - around)

    rows_out.wait_recv()

    def add_rows(row):
        for l in range(L):
            for c in range(C):
                out[l, c, row : row + 1, :] += 0.2 * row_recv[l * C + c : l * C + c + 1, :]

    pl.when(px == 0)(lambda: add_rows(X - 1))
    pl.when(px == 1)(lambda: add_rows(0))
    cols_out.wait_recv()
    at_edge = full_lane == jnp.where(py == 0, Y - 1, 0)
    for l in range(L):
        for c in range(C):
            i = l * C + c
            out[l, c] += jnp.where(at_edge, 0.2 * col_recv[:, i : i + 1], 0.0)

    for copy in spreads + sends + [send_prod, rows_out, cols_out]:
        copy.wait_send()
    for k in range(K):
        down_back_copy(k).wait_send()
        up_back_copy(k).wait_send()

    @pl.when(g < G - 1)
    def _():
        for k in range(K):
            down_copy(k).wait_send()

    @pl.when(g > 0)
    def _():
        for k in range(K):
            up_copy(k).wait_send()


def shards(source, phase, attenuation, pml_level, recv_values, recv_slab, recv_lateral, recv_layer):
    L, C, X, Y = source.shape
    S = lax.axis_size("slab")
    rows = recv_values.shape[3]
    K = CHUNKS
    H = X // 2
    R = H // K
    vmem, dma = pltpu.VMEM, pltpu.SemaphoreType.DMA
    chunked = vmem((K, C, R, Y), F32)
    scratch = [
        vmem((L, C, X, Y), F32), vmem((L, X, Y), F32), vmem((L, X, Y), F32), vmem((X, Y), jnp.int32),
        vmem((L, X, Y), F32), vmem((L, X, Y), F32),
        vmem((8, rows), F32), vmem((S, 8, LANES), F32), vmem((S, 8, LANES), F32),
        vmem((L * X, 3 * S * CAP), BF16), vmem((C * Y, 3 * S * CAP), BF16),
        vmem((2, H, Y), F32), vmem((2, 2, H, Y), F32),
        vmem((K, 2 * C, R, Y), F32), vmem((2, K, 2 * C, R, Y), F32),
        chunked, chunked, chunked, chunked,
        chunked, chunked, vmem((2, K, C, R, Y), F32), vmem((2, K, C, R, Y), F32),
        vmem((L, C, X + 16, Y), F32),
        vmem((L * C, Y), F32), vmem((L * C, Y), F32), vmem((X, LANES), F32), vmem((X, LANES), F32),
        dma((4,)), dma((S,)), dma((S,)), dma, dma, dma((K,)), dma((K,)),
        dma((K,)), dma((K,)), dma((K,)), dma((K,)), dma((K,)), dma((K,)), dma((K,)), dma((K,)),
        dma, dma, dma, dma,
    ]
    any_space = pl.BlockSpec(memory_space=pl.ANY)
    in_vmem = pl.BlockSpec(memory_space=pltpu.VMEM)
    return pl.pallas_call(
        functools.partial(kernel, (S, L, C, X, Y, K)),
        out_shape=jax.ShapeDtypeStruct(source.shape, F32),
        in_specs=[any_space] * 4 + [in_vmem] * 4,
        out_specs=in_vmem,
        scratch_shapes=scratch,
        compiler_params=pltpu.CompilerParams(
            collective_id=0, has_side_effects=True, vmem_limit_bytes=48 * 1024 * 1024
        ),
    )(
        source, phase, attenuation, pml_level,
        recv_values[0, 0], recv_slab[0, 0], recv_lateral[0], recv_layer[0],
    )


def solution(mesh):
    in_specs = (
        P("slab", None, "px", "py"),
        P("slab", "px", "py"),
        P("slab", "px", "py"),
        P("px", "py"),
        P("px", "py", None, "slab"),
        P("px", "py", "slab", None),
        P("px", "py", "slab"),
        P("px", "py", "slab"),
    )
    out_specs = P("slab", None, "px", "py")
    return jax.shard_map(shards, mesh=mesh, in_specs=in_specs, out_specs=out_specs, check_vma=False)
```

```python
import functools

import jax
import jax.numpy as jnp
from jax import lax
from jax.experimental import pallas as pl
from jax.experimental.pallas import tpu as pltpu
from jax.sharding import PartitionSpec as P

CHUNKS = 4
LANES = 128
CAP = 64
VMEM_BYTES = 60 * 1024 * 1024
BF16 = jnp.bfloat16
F32 = jnp.float32


def thirds(value):
    high = value.astype(BF16)
    rest = value - high.astype(F32)
    mid = rest.astype(BF16)
    low = (rest - mid.astype(F32)).astype(BF16)
    return high, mid, low


def times(rate, state):
    return rate[0] * state[0] - rate[1] * state[1], rate[0] * state[1] + rate[1] * state[0]


def circle(angle):
    t = (angle - 1.5707963705062866) + 4.371139000186241e-08
    z = t * t
    odd = -1.0 / 39916800.0
    for factor in (1.0 / 362880.0, -1.0 / 5040.0, 1.0 / 120.0, -1.0 / 6.0):
        odd = odd * z + factor
    even = 1.0 / 479001600.0
    for factor in (-1.0 / 3628800.0, 1.0 / 40320.0, -1.0 / 720.0, 1.0 / 24.0, -0.5):
        even = even * z + factor
    return -(t + t * z * odd), 1.0 + z * even


def kernel(
    sizes,
    src_hbm, phase_hbm, att_hbm, pml_hbm, vals_hbm, slab_hbm, lat_hbm, lay_hbm,
    out,
    vals, rslab, rlat, rlay, force, phase, att, pml, rate_re, rate_im,
    data, spread, arrived, right,
    prod_send, prod_pair, fwd_send, pair,
    down_send, down_recv, up_send, up_recv,
    down_back, up_back, enter_down, enter_up,
    comb, row_send, row_recv, col_send, col_recv,
    in_sem, spread_s, spread_r, prod_s, prod_r, fwd_s, fwd_r,
    down_s, down_r, up_s, up_r, dback_s, dback_r, uback_s, uback_r,
    row_s, row_r, col_s, col_r,
):
    S, L, C, X, Y, K = sizes
    G = S // 2
    H = X // 2
    R = H // K
    shots = C // 2
    me = lax.axis_index("slab")
    px = lax.axis_index("px")
    py = lax.axis_index("py")
    g = lax.div(me, 2)
    y = lax.rem(me, 2)
    partner = {"slab": g * 2 + (1 - y)}
    other_x = {"px": 1 - px}
    other_y = {"py": 1 - py}

    def remote(src, dst, send, recv, where):
        return pltpu.make_async_remote_copy(
            src_ref=src, dst_ref=dst, send_sem=send, recv_sem=recv,
            device_id=where, device_id_type=pl.DeviceIdType.MESH,
        )

    barrier = pltpu.get_barrier_semaphore()
    peers = [lax.rem(me + step, S) for step in range(1, S)]
    for where in [{"slab": peer} for peer in peers] + [other_x, other_y]:
        pl.semaphore_signal(barrier, inc=1, device_id=where, device_id_type=pl.DeviceIdType.MESH)

    loads = [
        pltpu.make_async_copy(a, b, in_sem.at[i])
        for i, (a, b) in enumerate(
            (
                (slab_hbm, rslab), (vals_hbm, vals), (lat_hbm, rlat), (lay_hbm, rlay),
                (phase_hbm, phase), (att_hbm, att), (pml_hbm, pml), (src_hbm, force),
            )
        )
    ]
    for load in loads:
        load.start()

    for load in loads[:4]:
        load.wait()
    rows = vals.shape[1]
    blocks = rows // LANES
    slab_of = rslab[...]
    hot = jnp.where(lax.broadcasted_iota(jnp.int32, (S, rows), 0) == slab_of, 1.0, 0.0)
    cuts = [hot[:, i * LANES : (i + 1) * LANES] for i in range(blocks)]
    earlier = jnp.where(
        lax.broadcasted_iota(jnp.int32, (LANES, LANES), 0)
        < lax.broadcasted_iota(jnp.int32, (LANES, LANES), 1),
        1.0, 0.0,
    ).astype(BF16)
    within = jnp.dot(
        jnp.concatenate(cuts, axis=0).astype(BF16), earlier, preferred_element_type=F32
    )
    passed = jnp.zeros((S, 1), F32)
    ranks = []
    for i in range(blocks):
        ranks.append(
            jnp.sum((within[i * S : (i + 1) * S] + passed) * cuts[i], axis=0, keepdims=True)
        )
        passed = passed + jnp.sum(cuts[i], axis=1, keepdims=True)
    slot = slab_of * LANES + jnp.concatenate(ranks, axis=1).astype(jnp.int32)
    lateral = rlat[...]
    data[...] = jnp.zeros_like(data)
    data[0:C, :] = vals[...]
    data[C : C + 1, :] = (rlay[...] * X + lax.div(lateral, Y)).astype(F32)
    data[C + 1 : C + 2, :] = lax.rem(lateral, Y).astype(F32)
    pieces = jnp.concatenate([part.astype(F32) for part in thirds(data[...])], axis=0).astype(BF16)
    slot_at = lax.broadcasted_iota(jnp.int32, (LANES, rows), 0)

    def route(s, carry):
        place = jnp.where(slot_at + s * LANES == slot, 1.0, 0.0).astype(BF16)
        routed = lax.dot_general(
            pieces, place, (((1,), (1,)), ((), ())), preferred_element_type=F32
        )
        spread[s] = routed[0:8] + routed[8:16] + routed[16:24]
        return carry

    lax.fori_loop(0, S, route, 0)

    pl.semaphore_wait(barrier, S + 1)
    arrived[me] = spread[me]
    spreads = []
    for peer in peers:
        copy = remote(
            spread.at[peer], arrived.at[me], spread_s.at[peer], spread_r.at[me], {"slab": peer}
        )
        copy.start()
        spreads.append(copy)

    for load in loads[4:7]:
        load.wait()

    def rate(l, carry):
        damping = att[l] + (0.5 / (L * S)) * pml[...].astype(F32)
        amplitude = jnp.exp(-damping)
        cosine, sine = circle(phase[l])
        rate_re[l] = amplitude * cosine
        rate_im[l] = amplitude * sine
        return carry

    lax.fori_loop(0, L, rate, 0)

    def product(half):
        at = pl.ds(pl.multiple_of(half * H, H), H)
        total = (rate_re[0, at], rate_im[0, at])
        for l in range(1, L):
            total = times((rate_re[l, at], rate_im[l, at]), total)
        return total

    total = product(1 - y)
    prod_send[0] = total[0]
    prod_send[1] = total[1]
    send_prod = remote(prod_send, prod_pair.at[y], prod_s, prod_r, partner)
    send_prod.start()
    total = product(y)
    prod_pair[y, 0] = total[0]
    prod_pair[y, 1] = total[1]

    for peer in peers:
        remote(
            spread.at[peer], arrived.at[peer], spread_s.at[peer], spread_r.at[peer], {"slab": peer}
        ).wait_recv()
    slots = S * CAP
    got = jnp.concatenate(
        [arrived[2 * i] + pltpu.roll(arrived[2 * i + 1], CAP, 1) for i in range(S // 2)], axis=1
    )
    row_at = got[C : C + 1, :].astype(jnp.int32)
    col_at = got[C + 1 : C + 2, :].astype(jnp.int32)
    x_at = lax.broadcasted_iota(jnp.int32, (X, slots), 0)
    on_col = lax.broadcasted_iota(jnp.int32, (Y, slots), 0) == col_at
    parts = [part.astype(F32) for part in thirds(got)]
    for i in range(3):
        for c in range(C):
            right[c * Y : (c + 1) * Y, i * slots : (i + 1) * slots] = jnp.where(
                on_col, parts[i][c : c + 1, :], 0.0
            ).astype(BF16)
    loads[7].wait()

    def inject(l, carry):
        on_row = jnp.where(x_at + l * X == row_at, 1.0, 0.0).astype(BF16)
        added = lax.dot_general(
            jnp.concatenate([on_row] * 3, axis=1), right[...], (((1,), (1,)), ((), ())),
            preferred_element_type=F32,
        )
        for c in range(C):
            force[l, c] += added[:, c * Y : (c + 1) * Y]
        return carry

    lax.fori_loop(0, L, inject, 0)

    def local(half, k, dst):
        at = pl.ds(pl.multiple_of(half * H + k * R, R), R)
        rates = [(rate_re[l, at], rate_im[l, at]) for l in range(L)]
        for s in range(shots):
            f = [(force[l, 2 * s, at], force[l, 2 * s + 1, at]) for l in range(L)]
            w = f[0]
            for l in range(1, L):
                re, im = times(rates[l], w)
                w = (re + f[l][0], im + f[l][1])
            v = f[L - 1]
            for l in range(L - 2, -1, -1):
                re, im = times(rates[l], v)
                v = (re + f[l][0], im + f[l][1])
            dst[2 * s] = w[0]
            dst[2 * s + 1] = w[1]
            dst[C + 2 * s] = v[0]
            dst[C + 2 * s + 1] = v[1]

    def fwd_copy(k):
        return remote(fwd_send.at[k], pair.at[y, k], fwd_s.at[k], fwd_r.at[k], partner)

    def give(k, carry):
        local(1 - y, k, fwd_send.at[k])
        fwd_copy(k).start()
        return carry

    def keep(k, carry):
        local(y, k, pair.at[y, k])
        return carry

    lax.fori_loop(0, K, give, 0)
    lax.fori_loop(0, K, keep, 0)

    pad = comb.shape[1] // 2 - X // 2
    column = jnp.where(py == 0, Y - 1, 0)
    chunk_lane = lax.broadcasted_iota(jnp.int32, (R, LANES), 1)

    def full(half, k):
        row = half * H + k * R
        at = pl.ds(pl.multiple_of(row, R), R)
        to = pl.ds(pl.multiple_of(row + pad, 8), R)
        rates = [(rate_re[l, at], rate_im[l, at]) for l in range(L)]
        held = jnp.zeros((R, LANES), F32)
        for s in range(shots):
            i, j = 2 * s, 2 * s + 1
            f = [(force[l, i, at], force[l, j, at]) for l in range(L)]
            w = (enter_down[half, k, i], enter_down[half, k, j])
            downs = []
            for l in range(L):
                re, im = times(rates[l], w)
                w = (re + f[l][0], im + f[l][1])
                downs.append(w)
            v = (enter_up[half, k, i], enter_up[half, k, j])
            for l in range(L - 1, -1, -1):
                turn = times(rates[l], v)
                for a in (0, 1):
                    plane = l * C + i + a
                    value = downs[l][a] + turn[a]
                    comb[plane, to] = value
                    shift = lax.rem(plane + LANES - column, LANES)
                    held = jnp.where(chunk_lane == plane, pltpu.roll(value, shift, 1), held)
                v = (turn[0] + f[l][0], turn[1] + f[l][1])
        col_send[at] = held

    @pl.when(g == 0)
    def _():
        down_recv[...] = jnp.zeros_like(down_recv)

    @pl.when(g == G - 1)
    def _():
        up_recv[...] = jnp.zeros_like(up_recv)

    def down_copy(k):
        return remote(down_send.at[k], down_recv.at[k], down_s.at[k], down_r.at[k], {"slab": me + 2})

    def up_copy(k):
        return remote(up_send.at[k], up_recv.at[k], up_s.at[k], up_r.at[k], {"slab": me - 2})

    def down_back_copy(k):
        return remote(down_back.at[k], enter_down.at[y, k], dback_s.at[k], dback_r.at[k], partner)

    def up_back_copy(k):
        return remote(up_back.at[k], enter_up.at[y, k], uback_s.at[k], uback_r.at[k], partner)

    def factors(k, member):
        at = pl.ds(pl.multiple_of(k * R, R), R)
        return prod_pair[member, 0, at], prod_pair[member, 1, at]

    def hop(k, first, second, base, incoming, outgoing, own, theirs, own_direct):
        near, far = factors(k, first), factors(k, second)
        for s in range(shots):
            i, j = 2 * s, 2 * s + 1
            e = (incoming[k, i], incoming[k, j])
            re, im = times(near, e)
            q = (re + pair[first, k, base + i], im + pair[first, k, base + j])
            re, im = times(far, q)
            outgoing[k, i] = re + pair[second, k, base + i]
            outgoing[k, j] = im + pair[second, k, base + j]
            for a in (0, 1):
                own[y, k, 2 * s + a] = jnp.where(own_direct, e[a], q[a])
                theirs[k, 2 * s + a] = jnp.where(own_direct, q[a], e[a])

    send_prod.wait_recv()
    ready = jnp.maximum(g, G - 1 - g)

    def chain(t, carry):
        @pl.when(t < K)
        def _():
            remote(
                fwd_send.at[t], pair.at[1 - y, t], fwd_s.at[t], fwd_r.at[t], partner
            ).wait_recv()
        kd = t - g
        ku = t - (G - 1 - g)

        @pl.when((kd >= 0) & (kd < K))
        def _():
            @pl.when(g > 0)
            def _():
                remote(
                    down_send.at[kd], down_recv.at[kd], down_s.at[kd], down_r.at[kd], {"slab": me - 2}
                ).wait_recv()

            hop(kd, 0, 1, 0, down_recv, down_send, enter_down, down_back, y == 0)

            @pl.when(g < G - 1)
            def _():
                down_copy(kd).start()

            down_back_copy(kd).start()

        @pl.when((ku >= 0) & (ku < K))
        def _():
            @pl.when(g < G - 1)
            def _():
                remote(
                    up_send.at[ku], up_recv.at[ku], up_s.at[ku], up_r.at[ku], {"slab": me + 2}
                ).wait_recv()

            hop(ku, 1, 0, C, up_recv, up_send, enter_up, up_back, y == 1)

            @pl.when(g > 0)
            def _():
                up_copy(ku).start()

            up_back_copy(ku).start()

        ke = t - ready

        @pl.when((ke >= 0) & (ke < K))
        def _():
            full(y, ke)

        return carry

    lax.fori_loop(0, K + G - 1, chain, 0)

    def finish(k, carry):
        remote(
            down_back.at[k], enter_down.at[1 - y, k], dback_s.at[k], dback_r.at[k], partner
        ).wait_recv()
        remote(
            up_back.at[k], enter_up.at[1 - y, k], uback_s.at[k], uback_r.at[k], partner
        ).wait_recv()
        full(1 - y, k)
        return carry

    lax.fori_loop(0, K, finish, 0)

    cols_out = remote(col_send, col_recv, col_s, col_r, other_y)
    cols_out.start()
    planes = L * C

    def send_rows(row):
        for i in range(planes):
            row_send[i : i + 1, :] = comb[i, pad + row : pad + row + 1, :]

    pl.when(px == 0)(lambda: send_rows(X - 1))
    pl.when(px == 1)(lambda: send_rows(0))
    rows_out = remote(row_send, row_recv, row_s, row_r, other_x)
    rows_out.start()

    full_lane = lax.broadcasted_iota(jnp.int32, (X, Y), 1)

    def stencil(i, carry):
        comb[i, pad - 1 : pad, :] = jnp.zeros((1, Y), F32)
        comb[i, pad + X : pad + X + 1, :] = jnp.zeros((1, Y), F32)
        here = comb[i, pad : pad + X, :]
        around = comb[i, pad - 1 : pad - 1 + X, :] + comb[i, pad + 1 : pad + 1 + X, :]
        around += jnp.where(full_lane == 0, 0.0, pltpu.roll(here, 1, 1))
        around += jnp.where(full_lane == Y - 1, 0.0, pltpu.roll(here, Y - 1, 1))
        out[lax.div(i, C), lax.rem(i, C)] = here - 0.2 * (4.0 * here - around)
        return carry

    lax.fori_loop(0, planes, stencil, 0)
    cols_out.wait_recv()
    at_edge = full_lane == column

    def add_columns(i, carry):
        shift = lax.rem(column + LANES - i, LANES)
        moved = pltpu.roll(col_recv[...], shift, 1)
        out[lax.div(i, C), lax.rem(i, C)] += jnp.where(at_edge, 0.2 * moved, 0.0)
        return carry

    lax.fori_loop(0, planes, add_columns, 0)
    rows_out.wait_recv()

    def add_rows(row):
        for l in range(L):
            for c in range(C):
                out[l, c, row : row + 1, :] += 0.2 * row_recv[l * C + c : l * C + c + 1, :]

    pl.when(px == 0)(lambda: add_rows(X - 1))
    pl.when(px == 1)(lambda: add_rows(0))

    for copy in spreads + [send_prod, rows_out, cols_out]:
        copy.wait_send()
    for k in range(K):
        fwd_copy(k).wait_send()
        down_back_copy(k).wait_send()
        up_back_copy(k).wait_send()

    @pl.when(g < G - 1)
    def _():
        for k in range(K):
            down_copy(k).wait_send()

    @pl.when(g > 0)
    def _():
        for k in range(K):
            up_copy(k).wait_send()


def shards(source, phase, attenuation, pml_level, recv_values, recv_slab, recv_lateral, recv_layer):
    L, C, X, Y = source.shape
    S = lax.axis_size("slab")
    rows = recv_values.shape[3]
    K = CHUNKS
    H = X // 2
    R = H // K
    vmem, dma = pltpu.VMEM, pltpu.SemaphoreType.DMA
    chunked = vmem((K, C, R, Y), F32)
    scratch = [
        vmem((C, rows), F32), vmem((1, rows), jnp.int32), vmem((1, rows), jnp.int32), vmem((1, rows), jnp.int32),
        vmem((L, C, X, Y), F32), vmem((L, X, Y), F32), vmem((L, X, Y), F32), vmem((X, Y), jnp.int32),
        vmem((L, X, Y), F32), vmem((L, X, Y), F32),
        vmem((8, rows), F32), vmem((S, 8, LANES), F32), vmem((S, 8, LANES), F32),
        vmem((C * Y, 3 * S * CAP), BF16),
        vmem((2, H, Y), F32), vmem((2, 2, H, Y), F32),
        vmem((K, 2 * C, R, Y), F32), vmem((2, K, 2 * C, R, Y), F32),
        chunked, chunked, chunked, chunked,
        chunked, chunked, vmem((2, K, C, R, Y), F32), vmem((2, K, C, R, Y), F32),
        vmem((L * C, X + 16, Y), F32),
        vmem((L * C, Y), F32), vmem((L * C, Y), F32), vmem((X, LANES), F32), vmem((X, LANES), F32),
        dma((8,)), dma((S,)), dma((S,)), dma, dma, dma((K,)), dma((K,)),
        dma((K,)), dma((K,)), dma((K,)), dma((K,)), dma((K,)), dma((K,)), dma((K,)), dma((K,)),
        dma, dma, dma, dma,
    ]
    any_space = pl.BlockSpec(memory_space=pl.ANY)
    in_vmem = pl.BlockSpec(memory_space=pltpu.VMEM)
    return pl.pallas_call(
        functools.partial(kernel, (S, L, C, X, Y, K)),
        out_shape=jax.ShapeDtypeStruct(source.shape, F32),
        in_specs=[any_space] * 8,
        out_specs=in_vmem,
        scratch_shapes=scratch,
        compiler_params=pltpu.CompilerParams(
            collective_id=0, has_side_effects=True, vmem_limit_bytes=VMEM_BYTES
        ),
    )(
        source, phase, attenuation, pml_level,
        recv_values[0, 0], recv_slab.reshape(1, rows), recv_lateral[0], recv_layer[0],
    )


def solution(mesh):
    in_specs = (
        P("slab", None, "px", "py"),
        P("slab", "px", "py"),
        P("slab", "px", "py"),
        P("px", "py"),
        P("px", "py", None, "slab"),
        P("px", "py", "slab", None),
        P("px", "py", "slab"),
        P("px", "py", "slab"),
    )
    out_specs = P("slab", None, "px", "py")
    return jax.shard_map(shards, mesh=mesh, in_specs=in_specs, out_specs=out_specs, check_vma=False)
```

```python
import functools

import jax
import jax.numpy as jnp
from jax import lax
from jax.experimental import pallas as pl
from jax.experimental.pallas import tpu as pltpu
from jax.sharding import PartitionSpec as P

GROUP = 4
CHUNKS = 2
LANES = 128
CAP = 64
VMEM_BYTES = 48 * 1024 * 1024
BF16 = jnp.bfloat16
F32 = jnp.float32


def thirds(value):
    high = value.astype(BF16)
    rest = value - high.astype(F32)
    mid = rest.astype(BF16)
    low = (rest - mid.astype(F32)).astype(BF16)
    return high, mid, low


def times(rate, state):
    return rate[0] * state[0] - rate[1] * state[1], rate[0] * state[1] + rate[1] * state[0]


def circle(angle):
    t = (angle - 1.5707963705062866) + 4.371139000186241e-08
    z = t * t
    odd = -1.0 / 39916800.0
    for factor in (1.0 / 362880.0, -1.0 / 5040.0, 1.0 / 120.0, -1.0 / 6.0):
        odd = odd * z + factor
    even = 1.0 / 479001600.0
    for factor in (-1.0 / 3628800.0, 1.0 / 40320.0, -1.0 / 720.0, 1.0 / 24.0, -0.5):
        even = even * z + factor
    return -(t + t * z * odd), 1.0 + z * even


def kernel(
    sizes,
    src_hbm, phase_hbm, att_hbm, pml_hbm, vals_hbm, slab_hbm, lat_hbm, lay_hbm,
    out,
    vals, rslab, rlat, rlay, force, phase, att, pml, rate_re, rate_im,
    data, spread, arrived, right,
    prod_send, prod_all, fwd_send, gathered,
    down_send, down_recv, up_send, up_recv,
    down_back, up_back, enter_down, enter_up,
    comb, row_send, row_recv, col_send, col_recv,
    in_sem, spread_s, spread_r, prod_s, prod_r, fwd_s, fwd_r,
    down_s, down_r, up_s, up_r, dback_s, dback_r, uback_s, uback_r,
    row_s, row_r, col_s, col_r,
):
    S, L, C, X, Y, K, M = sizes
    G = S // M
    H = X // M
    R = H // K
    shots = C // 2
    me = lax.axis_index("slab")
    px = lax.axis_index("px")
    py = lax.axis_index("py")
    g = lax.div(me, M)
    m = lax.rem(me, M)
    fellows = M - 1
    other_x = {"px": 1 - px}
    other_y = {"py": 1 - py}

    def fellow(step):
        return lax.rem(m + step, M)

    def place_of(member):
        return {"slab": g * M + member}

    def remote(src, dst, send, recv, where):
        return pltpu.make_async_remote_copy(
            src_ref=src, dst_ref=dst, send_sem=send, recv_sem=recv,
            device_id=where, device_id_type=pl.DeviceIdType.MESH,
        )

    barrier = pltpu.get_barrier_semaphore()
    peers = [lax.rem(me + step, S) for step in range(1, S)]
    for where in [{"slab": peer} for peer in peers] + [other_x, other_y]:
        pl.semaphore_signal(barrier, inc=1, device_id=where, device_id_type=pl.DeviceIdType.MESH)

    loads = [
        pltpu.make_async_copy(a, b, in_sem.at[i])
        for i, (a, b) in enumerate(
            (
                (slab_hbm, rslab), (vals_hbm, vals), (lat_hbm, rlat), (lay_hbm, rlay),
                (phase_hbm, phase), (att_hbm, att), (pml_hbm, pml), (src_hbm, force),
            )
        )
    ]
    for load in loads:
        load.start()

    for load in loads[:4]:
        load.wait()
    rows = vals.shape[1]
    blocks = rows // LANES
    slab_of = rslab[...]
    hot = jnp.where(lax.broadcasted_iota(jnp.int32, (S, rows), 0) == slab_of, 1.0, 0.0)
    cuts = [hot[:, i * LANES : (i + 1) * LANES] for i in range(blocks)]
    earlier = jnp.where(
        lax.broadcasted_iota(jnp.int32, (LANES, LANES), 0)
        < lax.broadcasted_iota(jnp.int32, (LANES, LANES), 1),
        1.0, 0.0,
    ).astype(BF16)
    within = jnp.dot(
        jnp.concatenate(cuts, axis=0).astype(BF16), earlier, preferred_element_type=F32
    )
    passed = jnp.zeros((S, 1), F32)
    ranks = []
    for i in range(blocks):
        ranks.append(
            jnp.sum((within[i * S : (i + 1) * S] + passed) * cuts[i], axis=0, keepdims=True)
        )
        passed = passed + jnp.sum(cuts[i], axis=1, keepdims=True)
    slot = slab_of * LANES + jnp.concatenate(ranks, axis=1).astype(jnp.int32)
    lateral = rlat[...]
    data[...] = jnp.zeros_like(data)
    data[0:C, :] = vals[...]
    data[C : C + 1, :] = (rlay[...] * X + lax.div(lateral, Y)).astype(F32)
    data[C + 1 : C + 2, :] = lax.rem(lateral, Y).astype(F32)
    pieces = jnp.concatenate([part.astype(F32) for part in thirds(data[...])], axis=0).astype(BF16)
    slot_at = lax.broadcasted_iota(jnp.int32, (LANES, rows), 0)

    def route(s, carry):
        place = jnp.where(slot_at + s * LANES == slot, 1.0, 0.0).astype(BF16)
        routed = lax.dot_general(
            pieces, place, (((1,), (1,)), ((), ())), preferred_element_type=F32
        )
        spread[s] = routed[0:8] + routed[8:16] + routed[16:24]
        return carry

    lax.fori_loop(0, S, route, 0)

    pl.semaphore_wait(barrier, S + 1)
    arrived[me] = spread[me]
    spreads = []
    for peer in peers:
        copy = remote(
            spread.at[peer], arrived.at[me], spread_s.at[peer], spread_r.at[me], {"slab": peer}
        )
        copy.start()
        spreads.append(copy)

    for load in loads[4:7]:
        load.wait()

    def rate(l, carry):
        damping = att[l] + (0.5 / (L * S)) * pml[...].astype(F32)
        amplitude = jnp.exp(-damping)
        cosine, sine = circle(phase[l])
        rate_re[l] = amplitude * cosine
        rate_im[l] = amplitude * sine
        return carry

    lax.fori_loop(0, L, rate, 0)

    def product(half):
        at = pl.ds(pl.multiple_of(half * H, H), H)
        total = (rate_re[0, at], rate_im[0, at])
        for l in range(1, L):
            total = times((rate_re[l, at], rate_im[l, at]), total)
        return total

    def prod_copy(j, source):
        return remote(
            prod_send.at[j], prod_all.at[source], prod_s.at[j], prod_r.at[source], place_of(j)
        )

    def give_product(step, carry):
        j = fellow(step)
        total = product(j)
        prod_send[j, 0] = total[0]
        prod_send[j, 1] = total[1]
        prod_copy(j, m).start()
        return carry

    lax.fori_loop(1, M, give_product, 0)
    total = product(m)
    prod_all[m, 0] = total[0]
    prod_all[m, 1] = total[1]

    for peer in peers:
        remote(
            spread.at[peer], arrived.at[peer], spread_s.at[peer], spread_r.at[peer], {"slab": peer}
        ).wait_recv()
    slots = S * CAP
    got = jnp.concatenate(
        [arrived[2 * i] + pltpu.roll(arrived[2 * i + 1], CAP, 1) for i in range(S // 2)], axis=1
    )
    row_at = got[C : C + 1, :].astype(jnp.int32)
    col_at = got[C + 1 : C + 2, :].astype(jnp.int32)
    x_at = lax.broadcasted_iota(jnp.int32, (X, slots), 0)
    on_col = lax.broadcasted_iota(jnp.int32, (Y, slots), 0) == col_at
    parts = [part.astype(F32) for part in thirds(got)]
    for i in range(3):
        for c in range(C):
            right[c * Y : (c + 1) * Y, i * slots : (i + 1) * slots] = jnp.where(
                on_col, parts[i][c : c + 1, :], 0.0
            ).astype(BF16)
    loads[7].wait()

    def inject(l, carry):
        on_row = jnp.where(x_at + l * X == row_at, 1.0, 0.0).astype(BF16)
        added = lax.dot_general(
            jnp.concatenate([on_row] * 3, axis=1), right[...], (((1,), (1,)), ((), ())),
            preferred_element_type=F32,
        )
        for c in range(C):
            force[l, c] += added[:, c * Y : (c + 1) * Y]
        return carry

    lax.fori_loop(0, L, inject, 0)

    def local(half, k, dst):
        at = pl.ds(pl.multiple_of(half * H + k * R, R), R)
        rates = [(rate_re[l, at], rate_im[l, at]) for l in range(L)]
        for s in range(shots):
            f = [(force[l, 2 * s, at], force[l, 2 * s + 1, at]) for l in range(L)]
            w = f[0]
            for l in range(1, L):
                re, im = times(rates[l], w)
                w = (re + f[l][0], im + f[l][1])
            v = f[L - 1]
            for l in range(L - 2, -1, -1):
                re, im = times(rates[l], v)
                v = (re + f[l][0], im + f[l][1])
            dst[2 * s] = w[0]
            dst[2 * s + 1] = w[1]
            dst[C + 2 * s] = v[0]
            dst[C + 2 * s + 1] = v[1]

    def fwd_copy(j, k, source):
        return remote(
            fwd_send.at[j, k], gathered.at[source, k], fwd_s.at[j, k], fwd_r.at[source, k],
            place_of(j),
        )

    def give(i, carry):
        k, j = lax.div(i, fellows), fellow(1 + lax.rem(i, fellows))
        local(j, k, fwd_send.at[j, k])
        fwd_copy(j, k, m).start()
        return carry

    def keep(k, carry):
        local(m, k, gathered.at[m, k])
        return carry

    lax.fori_loop(0, K * fellows, give, 0)
    lax.fori_loop(0, K, keep, 0)

    pad = comb.shape[1] // 2 - X // 2
    column = jnp.where(py == 0, Y - 1, 0)
    chunk_lane = lax.broadcasted_iota(jnp.int32, (R, LANES), 1)

    def full(half, k):
        row = half * H + k * R
        at = pl.ds(pl.multiple_of(row, R), R)
        to = pl.ds(pl.multiple_of(row + pad, 8), R)
        rates = [(rate_re[l, at], rate_im[l, at]) for l in range(L)]
        held = jnp.zeros((R, LANES), F32)
        for s in range(shots):
            i, j = 2 * s, 2 * s + 1
            f = [(force[l, i, at], force[l, j, at]) for l in range(L)]
            w = (enter_down[half, k, i], enter_down[half, k, j])
            downs = []
            for l in range(L):
                re, im = times(rates[l], w)
                w = (re + f[l][0], im + f[l][1])
                downs.append(w)
            v = (enter_up[half, k, i], enter_up[half, k, j])
            for l in range(L - 1, -1, -1):
                turn = times(rates[l], v)
                for a in (0, 1):
                    plane = l * C + i + a
                    value = downs[l][a] + turn[a]
                    comb[plane, to] = value
                    shift = lax.rem(plane + LANES - column, LANES)
                    held = jnp.where(chunk_lane == plane, pltpu.roll(value, shift, 1), held)
                v = (turn[0] + f[l][0], turn[1] + f[l][1])
        col_send[at] = held

    @pl.when(g == 0)
    def _():
        down_recv[...] = jnp.zeros_like(down_recv)

    @pl.when(g == G - 1)
    def _():
        up_recv[...] = jnp.zeros_like(up_recv)

    def down_copy(k, to):
        return remote(down_send.at[k], down_recv.at[k], down_s.at[k], down_r.at[k], {"slab": to})

    def up_copy(k, to):
        return remote(up_send.at[k], up_recv.at[k], up_s.at[k], up_r.at[k], {"slab": to})

    def down_back_copy(j, k, source):
        return remote(
            down_back.at[j, k], enter_down.at[source, k], dback_s.at[j, k], dback_r.at[source, k],
            place_of(j),
        )

    def up_back_copy(j, k, source):
        return remote(
            up_back.at[j, k], enter_up.at[source, k], uback_s.at[j, k], uback_r.at[source, k],
            place_of(j),
        )

    def hop(k, order, base, incoming, outgoing, back, own):
        at = pl.ds(pl.multiple_of(k * R, R), R)
        for s in range(shots):
            i, j = 2 * s, 2 * s + 1
            e = (incoming[k, i], incoming[k, j])
            for member in order:
                back[member, k, i] = e[0]
                back[member, k, j] = e[1]
                re, im = times((prod_all[member, 0, at], prod_all[member, 1, at]), e)
                e = (re + gathered[member, k, base + i], im + gathered[member, k, base + j])
            outgoing[k, i] = e[0]
            outgoing[k, j] = e[1]
        own[m, k] = back[m, k]

    def take_products(step, carry):
        j = fellow(step)
        prod_copy(j, j).wait_recv()
        return carry

    lax.fori_loop(1, M, take_products, 0)
    ready = jnp.maximum(g, G - 1 - g)

    def chain(t, carry):
        @pl.when(t < K)
        def _():
            for step in range(1, M):
                j = fellow(step)
                fwd_copy(j, t, j).wait_recv()

        kd = t - g
        ku = t - (G - 1 - g)
        has_down = (kd >= 0) & (kd < K)
        has_up = (ku >= 0) & (ku < K)

        @pl.when(has_down)
        def _():
            @pl.when(g > 0)
            def _():
                down_copy(kd, me - M).wait_recv()

            hop(kd, range(M), 0, down_recv, down_send, down_back, enter_down)

            @pl.when(g < G - 1)
            def _():
                down_copy(kd, me + M).start()

            for step in range(1, M):
                down_back_copy(fellow(step), kd, m).start()

        @pl.when(has_up)
        def _():
            @pl.when(g < G - 1)
            def _():
                up_copy(ku, me + M).wait_recv()

            hop(ku, range(M - 1, -1, -1), C, up_recv, up_send, up_back, enter_up)

            @pl.when(g > 0)
            def _():
                up_copy(ku, me - M).start()

            for step in range(1, M):
                up_back_copy(fellow(step), ku, m).start()

        ke = t - ready

        @pl.when((ke >= 0) & (ke < K))
        def _():
            full(m, ke)

        return carry

    lax.fori_loop(0, K + G - 1, chain, 0)

    def finish(i, carry):
        k, j = lax.div(i, fellows), fellow(1 + lax.rem(i, fellows))
        down_back_copy(j, k, j).wait_recv()
        up_back_copy(j, k, j).wait_recv()
        full(j, k)
        return carry

    lax.fori_loop(0, K * fellows, finish, 0)

    cols_out = remote(col_send, col_recv, col_s, col_r, other_y)
    cols_out.start()
    planes = L * C

    def send_rows(row):
        for i in range(planes):
            row_send[i : i + 1, :] = comb[i, pad + row : pad + row + 1, :]

    pl.when(px == 0)(lambda: send_rows(X - 1))
    pl.when(px == 1)(lambda: send_rows(0))
    rows_out = remote(row_send, row_recv, row_s, row_r, other_x)
    rows_out.start()

    full_lane = lax.broadcasted_iota(jnp.int32, (X, Y), 1)

    def stencil(i, carry):
        comb[i, pad - 1 : pad, :] = jnp.zeros((1, Y), F32)
        comb[i, pad + X : pad + X + 1, :] = jnp.zeros((1, Y), F32)
        here = comb[i, pad : pad + X, :]
        around = comb[i, pad - 1 : pad - 1 + X, :] + comb[i, pad + 1 : pad + 1 + X, :]
        around += jnp.where(full_lane == 0, 0.0, pltpu.roll(here, 1, 1))
        around += jnp.where(full_lane == Y - 1, 0.0, pltpu.roll(here, Y - 1, 1))
        out[lax.div(i, C), lax.rem(i, C)] = here - 0.2 * (4.0 * here - around)
        return carry

    lax.fori_loop(0, planes, stencil, 0)
    cols_out.wait_recv()
    at_edge = full_lane == column

    def add_columns(i, carry):
        shift = lax.rem(column + LANES - i, LANES)
        moved = pltpu.roll(col_recv[...], shift, 1)
        out[lax.div(i, C), lax.rem(i, C)] += jnp.where(at_edge, 0.2 * moved, 0.0)
        return carry

    lax.fori_loop(0, planes, add_columns, 0)
    rows_out.wait_recv()

    def add_rows(row):
        for l in range(L):
            for c in range(C):
                out[l, c, row : row + 1, :] += 0.2 * row_recv[l * C + c : l * C + c + 1, :]

    pl.when(px == 0)(lambda: add_rows(X - 1))
    pl.when(px == 1)(lambda: add_rows(0))

    for copy in spreads + [rows_out, cols_out]:
        copy.wait_send()

    def left(step, carry):
        j = fellow(step)
        prod_copy(j, m).wait_send()
        for k in range(K):
            fwd_copy(j, k, m).wait_send()
            down_back_copy(j, k, m).wait_send()
            up_back_copy(j, k, m).wait_send()
        return carry

    lax.fori_loop(1, M, left, 0)

    @pl.when(g < G - 1)
    def _():
        for k in range(K):
            down_copy(k, me + M).wait_send()

    @pl.when(g > 0)
    def _():
        for k in range(K):
            up_copy(k, me - M).wait_send()


def shards(source, phase, attenuation, pml_level, recv_values, recv_slab, recv_lateral, recv_layer):
    L, C, X, Y = source.shape
    S = lax.axis_size("slab")
    rows = recv_values.shape[3]
    K, M = CHUNKS, GROUP
    H = X // M
    R = H // K
    vmem, dma = pltpu.VMEM, pltpu.SemaphoreType.DMA
    chunked = vmem((K, C, R, Y), F32)
    spaced = vmem((M, K, C, R, Y), F32)
    scratch = [
        vmem((C, rows), F32), vmem((1, rows), jnp.int32), vmem((1, rows), jnp.int32), vmem((1, rows), jnp.int32),
        vmem((L, C, X, Y), F32), vmem((L, X, Y), F32), vmem((L, X, Y), F32), vmem((X, Y), jnp.int32),
        vmem((L, X, Y), F32), vmem((L, X, Y), F32),
        vmem((8, rows), F32), vmem((S, 8, LANES), F32), vmem((S, 8, LANES), F32),
        vmem((C * Y, 3 * S * CAP), BF16),
        vmem((M, 2, H, Y), F32), vmem((M, 2, H, Y), F32),
        vmem((M, K, 2 * C, R, Y), F32), vmem((M, K, 2 * C, R, Y), F32),
        chunked, chunked, chunked, chunked, spaced, spaced, spaced, spaced,
        vmem((L * C, X + 16, Y), F32),
        vmem((L * C, Y), F32), vmem((L * C, Y), F32), vmem((X, LANES), F32), vmem((X, LANES), F32),
        dma((8,)), dma((S,)), dma((S,)), dma((M,)), dma((M,)), dma((M, K)), dma((M, K)),
        dma((K,)), dma((K,)), dma((K,)), dma((K,)),
        dma((M, K)), dma((M, K)), dma((M, K)), dma((M, K)),
        dma, dma, dma, dma,
    ]
    in_hbm = pl.BlockSpec(memory_space=pltpu.HBM)
    in_vmem = pl.BlockSpec(memory_space=pltpu.VMEM)
    return pl.pallas_call(
        functools.partial(kernel, (S, L, C, X, Y, K, M)),
        out_shape=jax.ShapeDtypeStruct(source.shape, F32),
        in_specs=[in_hbm] * 8,
        out_specs=in_vmem,
        scratch_shapes=scratch,
        compiler_params=pltpu.CompilerParams(
            collective_id=0, has_side_effects=True, vmem_limit_bytes=VMEM_BYTES
        ),
    )(*(
        pltpu.with_memory_space_constraint(x, pltpu.HBM)
        for x in (
            source, phase, attenuation, pml_level,
            recv_values[0, 0], recv_slab.reshape(1, rows), recv_lateral[0], recv_layer[0],
        )
    ))


def solution(mesh):
    in_specs = (
        P("slab", None, "px", "py"),
        P("slab", "px", "py"),
        P("slab", "px", "py"),
        P("px", "py"),
        P("px", "py", None, "slab"),
        P("px", "py", "slab", None),
        P("px", "py", "slab"),
        P("px", "py", "slab"),
    )
    out_specs = P("slab", None, "px", "py")
    return jax.shard_map(shards, mesh=mesh, in_specs=in_specs, out_specs=out_specs, check_vma=False)
```

```python
import functools

import jax
import jax.numpy as jnp
from jax import lax
from jax.experimental import pallas as pl
from jax.experimental.pallas import tpu as pltpu
from jax.sharding import PartitionSpec as P

GROUP = 4
CHUNKS = 2
LANES = 128
CAP = 64
VMEM_BYTES = 48 * 1024 * 1024
BF16 = jnp.bfloat16
F32 = jnp.float32


def thirds(value):
    high = value.astype(BF16)
    rest = value - high.astype(F32)
    mid = rest.astype(BF16)
    low = (rest - mid.astype(F32)).astype(BF16)
    return high, mid, low


def times(rate, state):
    return rate[0] * state[0] - rate[1] * state[1], rate[0] * state[1] + rate[1] * state[0]


def circle(angle):
    t = (angle - 1.5707963705062866) + 4.371139000186241e-08
    z = t * t
    odd = -1.0 / 39916800.0
    for factor in (1.0 / 362880.0, -1.0 / 5040.0, 1.0 / 120.0, -1.0 / 6.0):
        odd = odd * z + factor
    even = 1.0 / 479001600.0
    for factor in (-1.0 / 3628800.0, 1.0 / 40320.0, -1.0 / 720.0, 1.0 / 24.0, -0.5):
        even = even * z + factor
    return -(t + t * z * odd), 1.0 + z * even


def kernel(
    sizes,
    src_hbm, phase_hbm, att_hbm, pml_hbm, vals_hbm, slab_hbm, lat_hbm, lay_hbm,
    out,
    vals, rslab, rlat, rlay, force, phase, att, pml, rate_re, rate_im,
    data, spread, arrived, left, right,
    prod_send, prod_all, fwd_send, gathered,
    down_send, down_recv, up_send, up_recv,
    down_back, up_back, enter_down, enter_up,
    comb, row_send, row_recv, col_send, col_recv,
    in_sem, spread_s, spread_r, prod_s, prod_r, fwd_s, fwd_r,
    down_s, down_r, up_s, up_r, dback_s, dback_r, uback_s, uback_r,
    row_s, row_r, col_s, col_r,
):
    S, L, C, X, Y, K, M = sizes
    G = S // M
    H = X // M
    R = H // K
    shots = C // 2
    me = lax.axis_index("slab")
    px = lax.axis_index("px")
    py = lax.axis_index("py")
    g = lax.div(me, M)
    m = lax.rem(me, M)
    fellows = M - 1
    other_x = {"px": 1 - px}
    other_y = {"py": 1 - py}

    def fellow(step):
        return lax.rem(m + step, M)

    def place_of(member):
        return {"slab": g * M + member}

    def remote(src, dst, send, recv, where):
        return pltpu.make_async_remote_copy(
            src_ref=src, dst_ref=dst, send_sem=send, recv_sem=recv,
            device_id=where, device_id_type=pl.DeviceIdType.MESH,
        )

    barrier = pltpu.get_barrier_semaphore()
    peers = [lax.rem(me + step, S) for step in range(1, S)]
    for where in [{"slab": peer} for peer in peers] + [other_x, other_y]:
        pl.semaphore_signal(barrier, inc=1, device_id=where, device_id_type=pl.DeviceIdType.MESH)

    loads = [
        pltpu.make_async_copy(a, b, in_sem.at[i])
        for i, (a, b) in enumerate(
            (
                (slab_hbm, rslab), (vals_hbm, vals), (lat_hbm, rlat), (lay_hbm, rlay),
                (phase_hbm, phase), (att_hbm, att), (pml_hbm, pml), (src_hbm, force),
            )
        )
    ]
    for load in loads:
        load.start()

    for load in loads[:4]:
        load.wait()
    rows = vals.shape[1]
    blocks = rows // LANES
    slab_of = rslab[...]
    hot = jnp.where(lax.broadcasted_iota(jnp.int32, (S, rows), 0) == slab_of, 1.0, 0.0)
    cuts = [hot[:, i * LANES : (i + 1) * LANES] for i in range(blocks)]
    earlier = jnp.where(
        lax.broadcasted_iota(jnp.int32, (LANES, LANES), 0)
        < lax.broadcasted_iota(jnp.int32, (LANES, LANES), 1),
        1.0, 0.0,
    ).astype(BF16)
    within = jnp.dot(
        jnp.concatenate(cuts, axis=0).astype(BF16), earlier, preferred_element_type=F32
    )
    passed = jnp.zeros((S, 1), F32)
    ranks = []
    for i in range(blocks):
        ranks.append(
            jnp.sum((within[i * S : (i + 1) * S] + passed) * cuts[i], axis=0, keepdims=True)
        )
        passed = passed + jnp.sum(cuts[i], axis=1, keepdims=True)
    slot = slab_of * CAP + jnp.concatenate(ranks, axis=1).astype(jnp.int32)
    lateral = rlat[...]
    data[...] = jnp.zeros_like(data)
    data[0:C, :] = vals[...]
    data[C : C + 1, :] = (rlay[...] * X + lax.div(lateral, Y)).astype(F32)
    data[C + 1 : C + 2, :] = lax.rem(lateral, Y).astype(F32)
    pieces = jnp.concatenate([part.astype(F32) for part in thirds(data[...])], axis=0).astype(BF16)
    slot_at = lax.broadcasted_iota(jnp.int32, (LANES, rows), 0)

    def route(s, carry):
        place = jnp.where(slot_at + s * LANES == slot, 1.0, 0.0).astype(BF16)
        routed = lax.dot_general(
            pieces, place, (((1,), (1,)), ((), ())), preferred_element_type=F32
        )
        spread[s] = routed[0:8] + routed[8:16] + routed[16:24]
        return carry

    lax.fori_loop(0, S // 2, route, 0, unroll=4)

    pl.semaphore_wait(barrier, S + 1)
    arrived[me] = spread[lax.div(me, 2)]
    spreads = []
    for peer in peers:
        copy = remote(
            spread.at[lax.div(peer, 2)], arrived.at[me], spread_s.at[peer], spread_r.at[me], {"slab": peer}
        )
        copy.start()
        spreads.append(copy)

    for load in loads[4:7]:
        load.wait()

    def rate(l, carry):
        damping = att[l] + (0.5 / (L * S)) * pml[...].astype(F32)
        amplitude = jnp.exp(-damping)
        cosine, sine = circle(phase[l])
        rate_re[l] = amplitude * cosine
        rate_im[l] = amplitude * sine
        return carry

    lax.fori_loop(0, L, rate, 0)

    def product(half):
        at = pl.ds(pl.multiple_of(half * H, H), H)
        total = (rate_re[0, at], rate_im[0, at])
        for l in range(1, L):
            total = times((rate_re[l, at], rate_im[l, at]), total)
        return total

    def prod_copy(j, source):
        return remote(
            prod_send.at[j], prod_all.at[source], prod_s.at[j], prod_r.at[source], place_of(j)
        )

    def give_product(step, carry):
        j = fellow(step)
        total = product(j)
        prod_send[j, 0] = total[0]
        prod_send[j, 1] = total[1]
        prod_copy(j, m).start()
        return carry

    lax.fori_loop(1, M, give_product, 0)
    total = product(m)
    prod_all[m, 0] = total[0]
    prod_all[m, 1] = total[1]

    for peer in peers:
        remote(
            spread.at[lax.div(peer, 2)], arrived.at[peer], spread_s.at[peer], spread_r.at[peer], {"slab": peer}
        ).wait_recv()
    slots = S * CAP
    low_half = lax.broadcasted_iota(jnp.int32, (8, LANES), 1) < CAP
    keeps_low = lax.rem(me, 2) == 0

    def packed(i):
        a, b = arrived[2 * i], arrived[2 * i + 1]
        low = jnp.where(keeps_low, a, pltpu.roll(a, CAP, 1))
        high = jnp.where(keeps_low, pltpu.roll(b, CAP, 1), b)
        return jnp.where(low_half, low, high)

    got = jnp.concatenate([packed(i) for i in range(S // 2)], axis=1)
    row_at = got[C : C + 1, :].astype(jnp.int32)
    col_at = got[C + 1 : C + 2, :].astype(jnp.int32)
    left[...] = jnp.where(
        lax.broadcasted_iota(jnp.int32, (L * X, slots), 0) == row_at, 1.0, 0.0
    ).astype(BF16)
    on_col = lax.broadcasted_iota(jnp.int32, (Y, slots), 0) == col_at
    parts = [part.astype(F32) for part in thirds(got)]
    loads[7].wait()
    for s in range(shots):
        for i in range(3):
            for a in (0, 1):
                c = 2 * s + a
                right[c * Y : (c + 1) * Y, i * slots : (i + 1) * slots] = jnp.where(
                    on_col, parts[i][c : c + 1, :], 0.0
                ).astype(BF16)
        added = lax.dot_general(
            jnp.concatenate([left[...]] * 3, axis=1), right[2 * s * Y : (2 * s + 2) * Y, :],
            (((1,), (1,)), ((), ())), preferred_element_type=F32,
        )
        for l in range(L):
            for a in (0, 1):
                force[l, 2 * s + a] += added[l * X : (l + 1) * X, a * Y : (a + 1) * Y]

    def local(half, k, dst):
        at = pl.ds(pl.multiple_of(half * H + k * R, R), R)
        rates = [(rate_re[l, at], rate_im[l, at]) for l in range(L)]
        for s in range(shots):
            f = [(force[l, 2 * s, at], force[l, 2 * s + 1, at]) for l in range(L)]
            w = f[0]
            for l in range(1, L):
                re, im = times(rates[l], w)
                w = (re + f[l][0], im + f[l][1])
            v = f[L - 1]
            for l in range(L - 2, -1, -1):
                re, im = times(rates[l], v)
                v = (re + f[l][0], im + f[l][1])
            dst[2 * s] = w[0]
            dst[2 * s + 1] = w[1]
            dst[C + 2 * s] = v[0]
            dst[C + 2 * s + 1] = v[1]

    def fwd_copy(j, k, source):
        return remote(
            fwd_send.at[j, k], gathered.at[source, k], fwd_s.at[j, k], fwd_r.at[source, k],
            place_of(j),
        )

    def give(i, carry):
        k, j = lax.div(i, fellows), fellow(1 + lax.rem(i, fellows))
        local(j, k, fwd_send.at[j, k])
        fwd_copy(j, k, m).start()
        return carry

    def keep(k, carry):
        local(m, k, gathered.at[m, k])
        return carry

    lax.fori_loop(0, K * fellows, give, 0)
    lax.fori_loop(0, K, keep, 0)

    pad = comb.shape[1] // 2 - X // 2
    column = jnp.where(py == 0, Y - 1, 0)
    chunk_lane = lax.broadcasted_iota(jnp.int32, (R, LANES), 1)

    def full(half, k):
        row = half * H + k * R
        at = pl.ds(pl.multiple_of(row, R), R)
        to = pl.ds(pl.multiple_of(row + pad, 8), R)
        rates = [(rate_re[l, at], rate_im[l, at]) for l in range(L)]
        held = jnp.zeros((R, LANES), F32)
        for s in range(shots):
            i, j = 2 * s, 2 * s + 1
            f = [(force[l, i, at], force[l, j, at]) for l in range(L)]
            w = (enter_down[half, k, i], enter_down[half, k, j])
            downs = []
            for l in range(L):
                re, im = times(rates[l], w)
                w = (re + f[l][0], im + f[l][1])
                downs.append(w)
            v = (enter_up[half, k, i], enter_up[half, k, j])
            for l in range(L - 1, -1, -1):
                turn = times(rates[l], v)
                for a in (0, 1):
                    plane = l * C + i + a
                    value = downs[l][a] + turn[a]
                    comb[plane, to] = value
                    shift = lax.rem(plane + LANES - column, LANES)
                    held = jnp.where(chunk_lane == plane, pltpu.roll(value, shift, 1), held)
                v = (turn[0] + f[l][0], turn[1] + f[l][1])
        col_send[at] = held

    @pl.when(g == 0)
    def _():
        down_recv[...] = jnp.zeros_like(down_recv)

    @pl.when(g == G - 1)
    def _():
        up_recv[...] = jnp.zeros_like(up_recv)

    def down_copy(k, to):
        return remote(down_send.at[k], down_recv.at[k], down_s.at[k], down_r.at[k], {"slab": to})

    def up_copy(k, to):
        return remote(up_send.at[k], up_recv.at[k], up_s.at[k], up_r.at[k], {"slab": to})

    def down_back_copy(j, k, source):
        return remote(
            down_back.at[j, k], enter_down.at[source, k], dback_s.at[j, k], dback_r.at[source, k],
            place_of(j),
        )

    def up_back_copy(j, k, source):
        return remote(
            up_back.at[j, k], enter_up.at[source, k], uback_s.at[j, k], uback_r.at[source, k],
            place_of(j),
        )

    def hop(k, order, base, incoming, outgoing, back, own):
        at = pl.ds(pl.multiple_of(k * R, R), R)
        for s in range(shots):
            i, j = 2 * s, 2 * s + 1
            e = (incoming[k, i], incoming[k, j])
            for member in order:
                back[member, k, i] = e[0]
                back[member, k, j] = e[1]
                re, im = times((prod_all[member, 0, at], prod_all[member, 1, at]), e)
                e = (re + gathered[member, k, base + i], im + gathered[member, k, base + j])
            outgoing[k, i] = e[0]
            outgoing[k, j] = e[1]
        own[m, k] = back[m, k]

    def take_products(step, carry):
        j = fellow(step)
        prod_copy(j, j).wait_recv()
        return carry

    lax.fori_loop(1, M, take_products, 0)
    ready = jnp.maximum(g, G - 1 - g)

    def chain(t, carry):
        @pl.when(t < K)
        def _():
            for step in range(1, M):
                j = fellow(step)
                fwd_copy(j, t, j).wait_recv()

        kd = t - g
        ku = t - (G - 1 - g)
        has_down = (kd >= 0) & (kd < K)
        has_up = (ku >= 0) & (ku < K)

        @pl.when(has_down)
        def _():
            @pl.when(g > 0)
            def _():
                down_copy(kd, me - M).wait_recv()

            hop(kd, range(M), 0, down_recv, down_send, down_back, enter_down)

            @pl.when(g < G - 1)
            def _():
                down_copy(kd, me + M).start()

            for step in range(1, M):
                down_back_copy(fellow(step), kd, m).start()

        @pl.when(has_up)
        def _():
            @pl.when(g < G - 1)
            def _():
                up_copy(ku, me + M).wait_recv()

            hop(ku, range(M - 1, -1, -1), C, up_recv, up_send, up_back, enter_up)

            @pl.when(g > 0)
            def _():
                up_copy(ku, me - M).start()

            for step in range(1, M):
                up_back_copy(fellow(step), ku, m).start()

        ke = t - ready

        @pl.when((ke >= 0) & (ke < K))
        def _():
            full(m, ke)

        return carry

    lax.fori_loop(0, K + G - 1, chain, 0)

    def finish(i, carry):
        k, j = lax.div(i, fellows), fellow(1 + lax.rem(i, fellows))
        down_back_copy(j, k, j).wait_recv()
        up_back_copy(j, k, j).wait_recv()
        full(j, k)
        return carry

    lax.fori_loop(0, K * fellows, finish, 0)

    cols_out = remote(col_send, col_recv, col_s, col_r, other_y)
    cols_out.start()
    planes = L * C

    def send_rows(row):
        for i in range(planes):
            row_send[i : i + 1, :] = comb[i, pad + row : pad + row + 1, :]

    pl.when(px == 0)(lambda: send_rows(X - 1))
    pl.when(px == 1)(lambda: send_rows(0))
    rows_out = remote(row_send, row_recv, row_s, row_r, other_x)
    rows_out.start()

    full_lane = lax.broadcasted_iota(jnp.int32, (X, Y), 1)

    def stencil(i, carry):
        comb[i, pad - 1 : pad, :] = jnp.zeros((1, Y), F32)
        comb[i, pad + X : pad + X + 1, :] = jnp.zeros((1, Y), F32)
        here = comb[i, pad : pad + X, :]
        around = comb[i, pad - 1 : pad - 1 + X, :] + comb[i, pad + 1 : pad + 1 + X, :]
        around += jnp.where(full_lane == 0, 0.0, pltpu.roll(here, 1, 1))
        around += jnp.where(full_lane == Y - 1, 0.0, pltpu.roll(here, Y - 1, 1))
        out[lax.div(i, C), lax.rem(i, C)] = here - 0.2 * (4.0 * here - around)
        return carry

    lax.fori_loop(0, planes, stencil, 0)
    cols_out.wait_recv()
    at_edge = full_lane == column

    def add_columns(i, carry):
        shift = lax.rem(column + LANES - i, LANES)
        moved = pltpu.roll(col_recv[...], shift, 1)
        out[lax.div(i, C), lax.rem(i, C)] += jnp.where(at_edge, 0.2 * moved, 0.0)
        return carry

    lax.fori_loop(0, planes, add_columns, 0)
    rows_out.wait_recv()

    def add_rows(row):
        for l in range(L):
            for c in range(C):
                out[l, c, row : row + 1, :] += 0.2 * row_recv[l * C + c : l * C + c + 1, :]

    pl.when(px == 0)(lambda: add_rows(X - 1))
    pl.when(px == 1)(lambda: add_rows(0))

    for copy in spreads + [rows_out, cols_out]:
        copy.wait_send()

    def drain(step, carry):
        j = fellow(step)
        prod_copy(j, m).wait_send()
        for k in range(K):
            fwd_copy(j, k, m).wait_send()
            down_back_copy(j, k, m).wait_send()
            up_back_copy(j, k, m).wait_send()
        return carry

    lax.fori_loop(1, M, drain, 0)

    @pl.when(g < G - 1)
    def _():
        for k in range(K):
            down_copy(k, me + M).wait_send()

    @pl.when(g > 0)
    def _():
        for k in range(K):
            up_copy(k, me - M).wait_send()


def shards(source, phase, attenuation, pml_level, recv_values, recv_slab, recv_lateral, recv_layer):
    L, C, X, Y = source.shape
    S = lax.axis_size("slab")
    rows = recv_values.shape[3]
    K, M = CHUNKS, GROUP
    H = X // M
    R = H // K
    vmem, dma = pltpu.VMEM, pltpu.SemaphoreType.DMA
    chunked = vmem((K, C, R, Y), F32)
    spaced = vmem((M, K, C, R, Y), F32)
    scratch = [
        vmem((C, rows), F32), vmem((1, rows), jnp.int32), vmem((1, rows), jnp.int32), vmem((1, rows), jnp.int32),
        vmem((L, C, X, Y), F32), vmem((L, X, Y), F32), vmem((L, X, Y), F32), vmem((X, Y), jnp.int32),
        vmem((L, X, Y), F32), vmem((L, X, Y), F32),
        vmem((8, rows), F32), vmem((S // 2, 8, LANES), F32), vmem((S, 8, LANES), F32),
        vmem((L * X, S * CAP), BF16), vmem((C * Y, 3 * S * CAP), BF16),
        vmem((M, 2, H, Y), F32), vmem((M, 2, H, Y), F32),
        vmem((M, K, 2 * C, R, Y), F32), vmem((M, K, 2 * C, R, Y), F32),
        chunked, chunked, chunked, chunked, spaced, spaced, spaced, spaced,
        vmem((L * C, X + 16, Y), F32),
        vmem((L * C, Y), F32), vmem((L * C, Y), F32), vmem((X, LANES), F32), vmem((X, LANES), F32),
        dma((8,)), dma((S,)), dma((S,)), dma((M,)), dma((M,)), dma((M, K)), dma((M, K)),
        dma((K,)), dma((K,)), dma((K,)), dma((K,)),
        dma((M, K)), dma((M, K)), dma((M, K)), dma((M, K)),
        dma, dma, dma, dma,
    ]
    in_hbm = pl.BlockSpec(memory_space=pltpu.HBM)
    in_vmem = pl.BlockSpec(memory_space=pltpu.VMEM)
    return pl.pallas_call(
        functools.partial(kernel, (S, L, C, X, Y, K, M)),
        out_shape=jax.ShapeDtypeStruct(source.shape, F32),
        in_specs=[in_hbm] * 8,
        out_specs=in_vmem,
        scratch_shapes=scratch,
        compiler_params=pltpu.CompilerParams(
            collective_id=0, has_side_effects=True, vmem_limit_bytes=VMEM_BYTES
        ),
    )(*(
        pltpu.with_memory_space_constraint(x, pltpu.HBM)
        for x in (
            source, phase, attenuation, pml_level,
            recv_values[0, 0], recv_slab.reshape(1, rows), recv_lateral[0], recv_layer[0],
        )
    ))


def solution(mesh):
    in_specs = (
        P("slab", None, "px", "py"),
        P("slab", "px", "py"),
        P("slab", "px", "py"),
        P("px", "py"),
        P("px", "py", None, "slab"),
        P("px", "py", "slab", None),
        P("px", "py", "slab"),
        P("px", "py", "slab"),
    )
    out_specs = P("slab", None, "px", "py")
    return jax.shard_map(shards, mesh=mesh, in_specs=in_specs, out_specs=out_specs, check_vma=False)
```

```python
import functools

import jax
import jax.numpy as jnp
from jax import lax
from jax.experimental import pallas as pl
from jax.experimental.pallas import tpu as pltpu
from jax.sharding import PartitionSpec as P

GROUP = 4
CHUNKS = 4
LANES = 128
CAP = 64
VMEM_BYTES = 48 * 1024 * 1024
BF16 = jnp.bfloat16
F32 = jnp.float32


def thirds(value):
    high = value.astype(BF16)
    rest = value - high.astype(F32)
    mid = rest.astype(BF16)
    low = (rest - mid.astype(F32)).astype(BF16)
    return high, mid, low


def times(rate, state):
    return rate[0] * state[0] - rate[1] * state[1], rate[0] * state[1] + rate[1] * state[0]


def circle(angle):
    t = (angle - 1.5707963705062866) + 4.371139000186241e-08
    z = t * t
    odd = -1.0 / 39916800.0
    for factor in (1.0 / 362880.0, -1.0 / 5040.0, 1.0 / 120.0, -1.0 / 6.0):
        odd = odd * z + factor
    even = 1.0 / 479001600.0
    for factor in (-1.0 / 3628800.0, 1.0 / 40320.0, -1.0 / 720.0, 1.0 / 24.0, -0.5):
        even = even * z + factor
    return -(t + t * z * odd), 1.0 + z * even


def kernel(
    sizes,
    src_hbm, phase_hbm, att_hbm, pml_hbm, vals_hbm, slab_hbm, lat_hbm, lay_hbm,
    out,
    vals, rslab, rlat, rlay, force, phase, att, pml, rate_re, rate_im,
    data, spread, arrived, left, right,
    prod_send, prod_all, fwd_send, gathered,
    down_send, down_recv, up_send, up_recv,
    down_back, up_back, enter_down, enter_up,
    comb, row_send, row_recv, col_send, col_recv,
    in_sem, spread_s, spread_r, prod_s, prod_r, fwd_s, fwd_r,
    down_s, down_r, up_s, up_r, dback_s, dback_r, uback_s, uback_r,
    row_s, row_r, col_s, col_r,
):
    S, L, C, X, Y, K, M = sizes
    G = S // M
    H = X // M
    R = H // K
    shots = C // 2
    me = lax.axis_index("slab")
    px = lax.axis_index("px")
    py = lax.axis_index("py")
    g = lax.div(me, M)
    m = lax.rem(me, M)
    fellows = M - 1
    other_x = {"px": 1 - px}
    other_y = {"py": 1 - py}

    def fellow(step):
        return lax.rem(m + step, M)

    def place_of(member):
        return {"slab": g * M + member}

    def remote(src, dst, send, recv, where):
        return pltpu.make_async_remote_copy(
            src_ref=src, dst_ref=dst, send_sem=send, recv_sem=recv,
            device_id=where, device_id_type=pl.DeviceIdType.MESH,
        )

    barrier = pltpu.get_barrier_semaphore()
    peers = [lax.rem(me + step, S) for step in range(1, S)]
    for where in [{"slab": peer} for peer in peers] + [other_x, other_y]:
        pl.semaphore_signal(barrier, inc=1, device_id=where, device_id_type=pl.DeviceIdType.MESH)

    loads = [
        pltpu.make_async_copy(a, b, in_sem.at[i])
        for i, (a, b) in enumerate(
            (
                (slab_hbm, rslab), (vals_hbm, vals), (lat_hbm, rlat), (lay_hbm, rlay),
                (phase_hbm, phase), (att_hbm, att), (pml_hbm, pml), (src_hbm, force),
            )
        )
    ]
    for load in loads:
        load.start()

    for load in loads[:4]:
        load.wait()
    rows = vals.shape[1]
    blocks = rows // LANES
    slab_of = rslab[...]
    hot = jnp.where(lax.broadcasted_iota(jnp.int32, (S, rows), 0) == slab_of, 1.0, 0.0)
    cuts = [hot[:, i * LANES : (i + 1) * LANES] for i in range(blocks)]
    earlier = jnp.where(
        lax.broadcasted_iota(jnp.int32, (LANES, LANES), 0)
        < lax.broadcasted_iota(jnp.int32, (LANES, LANES), 1),
        1.0, 0.0,
    ).astype(BF16)
    within = jnp.dot(
        jnp.concatenate(cuts, axis=0).astype(BF16), earlier, preferred_element_type=F32
    )
    passed = jnp.zeros((S, 1), F32)
    ranks = []
    for i in range(blocks):
        ranks.append(
            jnp.sum((within[i * S : (i + 1) * S] + passed) * cuts[i], axis=0, keepdims=True)
        )
        passed = passed + jnp.sum(cuts[i], axis=1, keepdims=True)
    slot = slab_of * CAP + jnp.concatenate(ranks, axis=1).astype(jnp.int32)
    lateral = rlat[...]
    data[...] = jnp.zeros_like(data)
    data[0:C, :] = vals[...]
    data[C : C + 1, :] = (rlay[...] * X + lax.div(lateral, Y)).astype(F32)
    data[C + 1 : C + 2, :] = lax.rem(lateral, Y).astype(F32)
    pieces = jnp.concatenate([part.astype(F32) for part in thirds(data[...])], axis=0).astype(BF16)
    slot_at = lax.broadcasted_iota(jnp.int32, (LANES, rows), 0)

    def route(s, carry):
        place = jnp.where(slot_at + s * LANES == slot, 1.0, 0.0).astype(BF16)
        routed = lax.dot_general(
            pieces, place, (((1,), (1,)), ((), ())), preferred_element_type=F32
        )
        spread[s] = routed[0:8] + routed[8:16] + routed[16:24]
        return carry

    lax.fori_loop(0, S // 2, route, 0, unroll=4)

    pl.semaphore_wait(barrier, S + 1)
    arrived[me] = spread[lax.div(me, 2)]
    spreads = []
    for peer in peers:
        copy = remote(
            spread.at[lax.div(peer, 2)], arrived.at[me], spread_s.at[peer], spread_r.at[me], {"slab": peer}
        )
        copy.start()
        spreads.append(copy)

    for load in loads[4:7]:
        load.wait()

    def rate(l, carry):
        damping = att[l] + (0.5 / (L * S)) * pml[...].astype(F32)
        amplitude = jnp.exp(-damping)
        cosine, sine = circle(phase[l])
        rate_re[l] = amplitude * cosine
        rate_im[l] = amplitude * sine
        return carry

    lax.fori_loop(0, L, rate, 0)

    def product(half):
        at = pl.ds(pl.multiple_of(half * H, H), H)
        total = (rate_re[0, at], rate_im[0, at])
        for l in range(1, L):
            total = times((rate_re[l, at], rate_im[l, at]), total)
        return total

    def prod_copy(j, source):
        return remote(
            prod_send.at[j], prod_all.at[source], prod_s.at[j], prod_r.at[source], place_of(j)
        )

    def give_product(step, carry):
        j = fellow(step)
        total = product(j)
        prod_send[j, 0] = total[0]
        prod_send[j, 1] = total[1]
        prod_copy(j, m).start()
        return carry

    lax.fori_loop(1, M, give_product, 0)
    total = product(m)
    prod_all[m, 0] = total[0]
    prod_all[m, 1] = total[1]

    for peer in peers:
        remote(
            spread.at[lax.div(peer, 2)], arrived.at[peer], spread_s.at[peer], spread_r.at[peer], {"slab": peer}
        ).wait_recv()
    slots = S * CAP
    low_half = lax.broadcasted_iota(jnp.int32, (8, LANES), 1) < CAP
    keeps_low = lax.rem(me, 2) == 0

    def packed(i):
        a, b = arrived[2 * i], arrived[2 * i + 1]
        low = jnp.where(keeps_low, a, pltpu.roll(a, CAP, 1))
        high = jnp.where(keeps_low, pltpu.roll(b, CAP, 1), b)
        return jnp.where(low_half, low, high)

    got = jnp.concatenate([packed(i) for i in range(S // 2)], axis=1)
    row_at = got[C : C + 1, :].astype(jnp.int32)
    col_at = got[C + 1 : C + 2, :].astype(jnp.int32)
    left[...] = jnp.where(
        lax.broadcasted_iota(jnp.int32, (L * X, slots), 0) == row_at, 1.0, 0.0
    ).astype(BF16)
    on_col = lax.broadcasted_iota(jnp.int32, (Y, slots), 0) == col_at
    parts = [part.astype(F32) for part in thirds(got)]
    loads[7].wait()
    for s in range(shots):
        for i in range(3):
            for a in (0, 1):
                c = 2 * s + a
                right[c * Y : (c + 1) * Y, i * slots : (i + 1) * slots] = jnp.where(
                    on_col, parts[i][c : c + 1, :], 0.0
                ).astype(BF16)
        added = lax.dot_general(
            jnp.concatenate([left[...]] * 3, axis=1), right[2 * s * Y : (2 * s + 2) * Y, :],
            (((1,), (1,)), ((), ())), preferred_element_type=F32,
        )
        for l in range(L):
            for a in (0, 1):
                force[l, 2 * s + a] += added[l * X : (l + 1) * X, a * Y : (a + 1) * Y]

    def local(half, k, dst):
        at = pl.ds(pl.multiple_of(half * H + k * R, R), R)
        rates = [(rate_re[l, at], rate_im[l, at]) for l in range(L)]
        for s in range(shots):
            f = [(force[l, 2 * s, at], force[l, 2 * s + 1, at]) for l in range(L)]
            w = f[0]
            for l in range(1, L):
                re, im = times(rates[l], w)
                w = (re + f[l][0], im + f[l][1])
            v = f[L - 1]
            for l in range(L - 2, -1, -1):
                re, im = times(rates[l], v)
                v = (re + f[l][0], im + f[l][1])
            dst[2 * s] = w[0]
            dst[2 * s + 1] = w[1]
            dst[C + 2 * s] = v[0]
            dst[C + 2 * s + 1] = v[1]

    def fwd_copy(j, k, source):
        return remote(
            fwd_send.at[j, k], gathered.at[source, k], fwd_s.at[j, k], fwd_r.at[source, k],
            place_of(j),
        )

    def give(i, carry):
        k, j = lax.div(i, fellows), fellow(1 + lax.rem(i, fellows))
        local(j, k, fwd_send.at[j, k])
        fwd_copy(j, k, m).start()
        return carry

    def keep(k, carry):
        local(m, k, gathered.at[m, k])
        return carry

    lax.fori_loop(0, K * fellows, give, 0)
    lax.fori_loop(0, K, keep, 0)

    pad = comb.shape[1] // 2 - X // 2
    column = jnp.where(py == 0, Y - 1, 0)
    chunk_lane = lax.broadcasted_iota(jnp.int32, (R, LANES), 1)

    def full(half, k):
        row = half * H + k * R
        at = pl.ds(pl.multiple_of(row, R), R)
        to = pl.ds(pl.multiple_of(row + pad, 8), R)
        rates = [(rate_re[l, at], rate_im[l, at]) for l in range(L)]
        held = jnp.zeros((R, LANES), F32)
        for s in range(shots):
            i, j = 2 * s, 2 * s + 1
            f = [(force[l, i, at], force[l, j, at]) for l in range(L)]
            w = (enter_down[half, k, i], enter_down[half, k, j])
            downs = []
            for l in range(L):
                re, im = times(rates[l], w)
                w = (re + f[l][0], im + f[l][1])
                downs.append(w)
            v = (enter_up[half, k, i], enter_up[half, k, j])
            for l in range(L - 1, -1, -1):
                turn = times(rates[l], v)
                for a in (0, 1):
                    plane = l * C + i + a
                    value = downs[l][a] + turn[a]
                    comb[plane, to] = value
                    shift = lax.rem(plane + LANES - column, LANES)
                    held = jnp.where(chunk_lane == plane, pltpu.roll(value, shift, 1), held)
                v = (turn[0] + f[l][0], turn[1] + f[l][1])
        col_send[at] = held

    @pl.when(g == 0)
    def _():
        down_recv[...] = jnp.zeros_like(down_recv)

    @pl.when(g == G - 1)
    def _():
        up_recv[...] = jnp.zeros_like(up_recv)

    def down_copy(k, to):
        return remote(down_send.at[k], down_recv.at[k], down_s.at[k], down_r.at[k], {"slab": to})

    def up_copy(k, to):
        return remote(up_send.at[k], up_recv.at[k], up_s.at[k], up_r.at[k], {"slab": to})

    def down_back_copy(j, k, source):
        return remote(
            down_back.at[j, k], enter_down.at[source, k], dback_s.at[j, k], dback_r.at[source, k],
            place_of(j),
        )

    def up_back_copy(j, k, source):
        return remote(
            up_back.at[j, k], enter_up.at[source, k], uback_s.at[j, k], uback_r.at[source, k],
            place_of(j),
        )

    def hop(k, order, base, incoming, outgoing, back, own):
        at = pl.ds(pl.multiple_of(k * R, R), R)
        for s in range(shots):
            i, j = 2 * s, 2 * s + 1
            e = (incoming[k, i], incoming[k, j])
            for member in order:
                back[member, k, i] = e[0]
                back[member, k, j] = e[1]
                re, im = times((prod_all[member, 0, at], prod_all[member, 1, at]), e)
                e = (re + gathered[member, k, base + i], im + gathered[member, k, base + j])
            outgoing[k, i] = e[0]
            outgoing[k, j] = e[1]
        own[m, k] = back[m, k]

    def take_products(step, carry):
        j = fellow(step)
        prod_copy(j, j).wait_recv()
        return carry

    lax.fori_loop(1, M, take_products, 0)
    ready = jnp.maximum(g, G - 1 - g)

    def chain(t, carry):
        @pl.when(t < K)
        def _():
            for step in range(1, M):
                j = fellow(step)
                fwd_copy(j, t, j).wait_recv()

        kd = t - g
        ku = t - (G - 1 - g)
        has_down = (kd >= 0) & (kd < K)
        has_up = (ku >= 0) & (ku < K)

        @pl.when(has_down)
        def _():
            @pl.when(g > 0)
            def _():
                down_copy(kd, me - M).wait_recv()

            hop(kd, range(M), 0, down_recv, down_send, down_back, enter_down)

            @pl.when(g < G - 1)
            def _():
                down_copy(kd, me + M).start()

            for step in range(1, M):
                down_back_copy(fellow(step), kd, m).start()

        @pl.when(has_up)
        def _():
            @pl.when(g < G - 1)
            def _():
                up_copy(ku, me + M).wait_recv()

            hop(ku, range(M - 1, -1, -1), C, up_recv, up_send, up_back, enter_up)

            @pl.when(g > 0)
            def _():
                up_copy(ku, me - M).start()

            for step in range(1, M):
                up_back_copy(fellow(step), ku, m).start()

        ke = t - ready

        @pl.when((ke >= 0) & (ke < K))
        def _():
            full(m, ke)

        return carry

    lax.fori_loop(0, K + G - 1, chain, 0)

    def finish(i, carry):
        k, j = lax.div(i, fellows), fellow(1 + lax.rem(i, fellows))
        down_back_copy(j, k, j).wait_recv()
        up_back_copy(j, k, j).wait_recv()
        full(j, k)
        return carry

    lax.fori_loop(0, K * fellows, finish, 0)

    cols_out = remote(col_send, col_recv, col_s, col_r, other_y)
    cols_out.start()
    planes = L * C

    def send_rows(row):
        for i in range(planes):
            row_send[i : i + 1, :] = comb[i, pad + row : pad + row + 1, :]

    pl.when(px == 0)(lambda: send_rows(X - 1))
    pl.when(px == 1)(lambda: send_rows(0))
    rows_out = remote(row_send, row_recv, row_s, row_r, other_x)
    rows_out.start()

    full_lane = lax.broadcasted_iota(jnp.int32, (X, Y), 1)

    def stencil(i, carry):
        comb[i, pad - 1 : pad, :] = jnp.zeros((1, Y), F32)
        comb[i, pad + X : pad + X + 1, :] = jnp.zeros((1, Y), F32)
        here = comb[i, pad : pad + X, :]
        around = comb[i, pad - 1 : pad - 1 + X, :] + comb[i, pad + 1 : pad + 1 + X, :]
        around += jnp.where(full_lane == 0, 0.0, pltpu.roll(here, 1, 1))
        around += jnp.where(full_lane == Y - 1, 0.0, pltpu.roll(here, Y - 1, 1))
        out[lax.div(i, C), lax.rem(i, C)] = here - 0.2 * (4.0 * here - around)
        return carry

    lax.fori_loop(0, planes, stencil, 0)
    cols_out.wait_recv()
    at_edge = full_lane == column

    def add_columns(i, carry):
        shift = lax.rem(column + LANES - i, LANES)
        moved = pltpu.roll(col_recv[...], shift, 1)
        out[lax.div(i, C), lax.rem(i, C)] += jnp.where(at_edge, 0.2 * moved, 0.0)
        return carry

    lax.fori_loop(0, planes, add_columns, 0)
    rows_out.wait_recv()

    def add_rows(row):
        for l in range(L):
            for c in range(C):
                out[l, c, row : row + 1, :] += 0.2 * row_recv[l * C + c : l * C + c + 1, :]

    pl.when(px == 0)(lambda: add_rows(X - 1))
    pl.when(px == 1)(lambda: add_rows(0))

    for copy in spreads + [rows_out, cols_out]:
        copy.wait_send()

    def drain(step, carry):
        j = fellow(step)
        prod_copy(j, m).wait_send()
        for k in range(K):
            fwd_copy(j, k, m).wait_send()
            down_back_copy(j, k, m).wait_send()
            up_back_copy(j, k, m).wait_send()
        return carry

    lax.fori_loop(1, M, drain, 0)

    @pl.when(g < G - 1)
    def _():
        for k in range(K):
            down_copy(k, me + M).wait_send()

    @pl.when(g > 0)
    def _():
        for k in range(K):
            up_copy(k, me - M).wait_send()


def shards(source, phase, attenuation, pml_level, recv_values, recv_slab, recv_lateral, recv_layer):
    L, C, X, Y = source.shape
    S = lax.axis_size("slab")
    rows = recv_values.shape[3]
    K, M = CHUNKS, GROUP
    H = X // M
    R = H // K
    vmem, dma = pltpu.VMEM, pltpu.SemaphoreType.DMA
    chunked = vmem((K, C, R, Y), F32)
    spaced = vmem((M, K, C, R, Y), F32)
    scratch = [
        vmem((C, rows), F32), vmem((1, rows), jnp.int32), vmem((1, rows), jnp.int32), vmem((1, rows), jnp.int32),
        vmem((L, C, X, Y), F32), vmem((L, X, Y), F32), vmem((L, X, Y), F32), vmem((X, Y), jnp.int32),
        vmem((L, X, Y), F32), vmem((L, X, Y), F32),
        vmem((8, rows), F32), vmem((S // 2, 8, LANES), F32), vmem((S, 8, LANES), F32),
        vmem((L * X, S * CAP), BF16), vmem((C * Y, 3 * S * CAP), BF16),
        vmem((M, 2, H, Y), F32), vmem((M, 2, H, Y), F32),
        vmem((M, K, 2 * C, R, Y), F32), vmem((M, K, 2 * C, R, Y), F32),
        chunked, chunked, chunked, chunked, spaced, spaced, spaced, spaced,
        vmem((L * C, X + 16, Y), F32),
        vmem((L * C, Y), F32), vmem((L * C, Y), F32), vmem((X, LANES), F32), vmem((X, LANES), F32),
        dma((8,)), dma((S,)), dma((S,)), dma((M,)), dma((M,)), dma((M, K)), dma((M, K)),
        dma((K,)), dma((K,)), dma((K,)), dma((K,)),
        dma((M, K)), dma((M, K)), dma((M, K)), dma((M, K)),
        dma, dma, dma, dma,
    ]
    in_hbm = pl.BlockSpec(memory_space=pltpu.HBM)
    in_vmem = pl.BlockSpec(memory_space=pltpu.VMEM)
    return pl.pallas_call(
        functools.partial(kernel, (S, L, C, X, Y, K, M)),
        out_shape=jax.ShapeDtypeStruct(source.shape, F32),
        in_specs=[in_hbm] * 8,
        out_specs=in_vmem,
        scratch_shapes=scratch,
        compiler_params=pltpu.CompilerParams(
            collective_id=0, has_side_effects=True, vmem_limit_bytes=VMEM_BYTES
        ),
    )(*(
        pltpu.with_memory_space_constraint(x, pltpu.HBM)
        for x in (
            source, phase, attenuation, pml_level,
            recv_values[0, 0], recv_slab.reshape(1, rows), recv_lateral[0], recv_layer[0],
        )
    ))


def solution(mesh):
    in_specs = (
        P("slab", None, "px", "py"),
        P("slab", "px", "py"),
        P("slab", "px", "py"),
        P("px", "py"),
        P("px", "py", None, "slab"),
        P("px", "py", "slab", None),
        P("px", "py", "slab"),
        P("px", "py", "slab"),
    )
    out_specs = P("slab", None, "px", "py")
    return jax.shard_map(shards, mesh=mesh, in_specs=in_specs, out_specs=out_specs, check_vma=False)
```

```python
import functools

import jax
import jax.numpy as jnp
from jax import lax
from jax.experimental import pallas as pl
from jax.experimental.pallas import tpu as pltpu
from jax.sharding import PartitionSpec as P

GROUP = 4
CHUNKS = 2
LANES = 128
CAP = 64
VMEM_BYTES = 48 * 1024 * 1024
BF16 = jnp.bfloat16
F32 = jnp.float32


def thirds(value):
    high = value.astype(BF16)
    rest = value - high.astype(F32)
    mid = rest.astype(BF16)
    low = (rest - mid.astype(F32)).astype(BF16)
    return high, mid, low


def times(rate, state):
    return rate[0] * state[0] - rate[1] * state[1], rate[0] * state[1] + rate[1] * state[0]


def circle(angle):
    t = (angle - 1.5707963705062866) + 4.371139000186241e-08
    z = t * t
    odd = -1.0 / 39916800.0
    for factor in (1.0 / 362880.0, -1.0 / 5040.0, 1.0 / 120.0, -1.0 / 6.0):
        odd = odd * z + factor
    even = 1.0 / 479001600.0
    for factor in (-1.0 / 3628800.0, 1.0 / 40320.0, -1.0 / 720.0, 1.0 / 24.0, -0.5):
        even = even * z + factor
    return -(t + t * z * odd), 1.0 + z * even


def kernel(
    sizes,
    src_hbm, phase_hbm, att_hbm, pml_hbm, vals_hbm, slab_hbm, lat_hbm, lay_hbm,
    out,
    vals, rslab, rlat, rlay, force, phase, att, pml, rate_re, rate_im,
    data, spread, arrived, left, right,
    prod_send, prod_all, fwd_send, gathered,
    down_send, down_recv, up_send, up_recv,
    down_back, up_back, enter_down, enter_up,
    comb, row_send, row_recv, col_send, col_recv,
    in_sem, spread_s, spread_r, prod_s, prod_r, fwd_s, fwd_r,
    down_s, down_r, up_s, up_r, dback_s, dback_r, uback_s, uback_r,
    row_s, row_r, col_s, col_r,
):
    S, L, C, X, Y, K, M = sizes
    G = S // M
    H = X // M
    R = H // K
    shots = C // 2
    me = lax.axis_index("slab")
    px = lax.axis_index("px")
    py = lax.axis_index("py")
    g = lax.div(me, M)
    m = lax.rem(me, M)
    other_x = {"px": 1 - px}
    other_y = {"py": 1 - py}

    def fellow(step):
        return lax.rem(m + step, M)

    def place_of(member):
        return {"slab": g * M + member}

    def remote(src, dst, send, recv, where):
        return pltpu.make_async_remote_copy(
            src_ref=src, dst_ref=dst, send_sem=send, recv_sem=recv,
            device_id=where, device_id_type=pl.DeviceIdType.MESH,
        )

    barrier = pltpu.get_barrier_semaphore()
    peers = [lax.rem(me + step, S) for step in range(1, S)]
    for where in [{"slab": peer} for peer in peers] + [other_x, other_y]:
        pl.semaphore_signal(barrier, inc=1, device_id=where, device_id_type=pl.DeviceIdType.MESH)

    loads = [
        pltpu.make_async_copy(a, b, in_sem.at[i])
        for i, (a, b) in enumerate(
            (
                (slab_hbm, rslab), (vals_hbm, vals), (lat_hbm, rlat), (lay_hbm, rlay),
                (phase_hbm, phase), (att_hbm, att), (pml_hbm, pml), (src_hbm, force),
            )
        )
    ]
    for load in loads:
        load.start()

    for load in loads[:4]:
        load.wait()
    rows = vals.shape[1]
    blocks = rows // LANES
    slab_of = rslab[...]
    hot = jnp.where(lax.broadcasted_iota(jnp.int32, (S, rows), 0) == slab_of, 1.0, 0.0)
    cuts = [hot[:, i * LANES : (i + 1) * LANES] for i in range(blocks)]
    earlier = jnp.where(
        lax.broadcasted_iota(jnp.int32, (LANES, LANES), 0)
        < lax.broadcasted_iota(jnp.int32, (LANES, LANES), 1),
        1.0, 0.0,
    ).astype(BF16)
    within = jnp.dot(
        jnp.concatenate(cuts, axis=0).astype(BF16), earlier, preferred_element_type=F32
    )
    passed = jnp.zeros((S, 1), F32)
    ranks = []
    for i in range(blocks):
        ranks.append(
            jnp.sum((within[i * S : (i + 1) * S] + passed) * cuts[i], axis=0, keepdims=True)
        )
        passed = passed + jnp.sum(cuts[i], axis=1, keepdims=True)
    slot = slab_of * CAP + jnp.concatenate(ranks, axis=1).astype(jnp.int32)
    lateral = rlat[...]
    data[...] = jnp.zeros_like(data)
    data[0:C, :] = vals[...]
    data[C : C + 1, :] = (rlay[...] * X + lax.div(lateral, Y)).astype(F32)
    data[C + 1 : C + 2, :] = lax.rem(lateral, Y).astype(F32)
    pieces = jnp.concatenate([part.astype(F32) for part in thirds(data[...])], axis=0).astype(BF16)
    slot_at = lax.broadcasted_iota(jnp.int32, (LANES, rows), 0)

    def route(s, carry):
        place = jnp.where(slot_at + s * LANES == slot, 1.0, 0.0).astype(BF16)
        routed = lax.dot_general(
            pieces, place, (((1,), (1,)), ((), ())), preferred_element_type=F32
        )
        spread[s] = routed[0:8] + routed[8:16] + routed[16:24]
        return carry

    lax.fori_loop(0, S // 2, route, 0, unroll=4)

    pl.semaphore_wait(barrier, S + 1)
    arrived[me] = spread[lax.div(me, 2)]
    spreads = []
    for peer in peers:
        copy = remote(
            spread.at[lax.div(peer, 2)], arrived.at[me], spread_s.at[peer], spread_r.at[me], {"slab": peer}
        )
        copy.start()
        spreads.append(copy)

    for load in loads[4:7]:
        load.wait()

    def rate(l, carry):
        damping = att[l] + (0.5 / (L * S)) * pml[...].astype(F32)
        amplitude = jnp.exp(-damping)
        cosine, sine = circle(phase[l])
        rate_re[l] = amplitude * cosine
        rate_im[l] = amplitude * sine
        return carry

    lax.fori_loop(0, L, rate, 0)

    def product(half):
        at = pl.ds(pl.multiple_of(half * H, H), H)
        total = (rate_re[0, at], rate_im[0, at])
        for l in range(1, L):
            total = times((rate_re[l, at], rate_im[l, at]), total)
        return total

    def prod_copy(j, source):
        return remote(
            prod_send.at[j], prod_all.at[source], prod_s.at[j], prod_r.at[source], place_of(j)
        )

    def give_product(step, carry):
        j = fellow(step)
        total = product(j)
        prod_send[j, 0] = total[0]
        prod_send[j, 1] = total[1]
        prod_copy(j, m).start()
        return carry

    lax.fori_loop(1, M, give_product, 0)
    total = product(m)
    prod_all[m, 0] = total[0]
    prod_all[m, 1] = total[1]

    for peer in peers:
        remote(
            spread.at[lax.div(peer, 2)], arrived.at[peer], spread_s.at[peer], spread_r.at[peer], {"slab": peer}
        ).wait_recv()
    slots = S * CAP
    low_half = lax.broadcasted_iota(jnp.int32, (8, LANES), 1) < CAP
    keeps_low = lax.rem(me, 2) == 0

    def packed(i):
        a, b = arrived[2 * i], arrived[2 * i + 1]
        low = jnp.where(keeps_low, a, pltpu.roll(a, CAP, 1))
        high = jnp.where(keeps_low, pltpu.roll(b, CAP, 1), b)
        return jnp.where(low_half, low, high)

    got = jnp.concatenate([packed(i) for i in range(S // 2)], axis=1)
    row_at = got[C : C + 1, :].astype(jnp.int32)
    col_at = got[C + 1 : C + 2, :].astype(jnp.int32)
    left[...] = jnp.where(
        lax.broadcasted_iota(jnp.int32, (L * X, slots), 0) == row_at, 1.0, 0.0
    ).astype(BF16)
    on_col = lax.broadcasted_iota(jnp.int32, (Y, slots), 0) == col_at
    parts = [part.astype(F32) for part in thirds(got)]
    loads[7].wait()
    for s in range(shots):
        for i in range(3):
            for a in (0, 1):
                c = 2 * s + a
                right[c * Y : (c + 1) * Y, i * slots : (i + 1) * slots] = jnp.where(
                    on_col, parts[i][c : c + 1, :], 0.0
                ).astype(BF16)
        added = lax.dot_general(
            jnp.concatenate([left[...]] * 3, axis=1), right[2 * s * Y : (2 * s + 2) * Y, :],
            (((1,), (1,)), ((), ())), preferred_element_type=F32,
        )
        for l in range(L):
            for a in (0, 1):
                force[l, 2 * s + a] += added[l * X : (l + 1) * X, a * Y : (a + 1) * Y]

    def local(half, k, dst):
        at = pl.ds(pl.multiple_of(half * H + k * R, R), R)
        rates = [(rate_re[l, at], rate_im[l, at]) for l in range(L)]
        for s in range(shots):
            f = [(force[l, 2 * s, at], force[l, 2 * s + 1, at]) for l in range(L)]
            w = f[0]
            for l in range(1, L):
                re, im = times(rates[l], w)
                w = (re + f[l][0], im + f[l][1])
            v = f[L - 1]
            for l in range(L - 2, -1, -1):
                re, im = times(rates[l], v)
                v = (re + f[l][0], im + f[l][1])
            dst[2 * s] = w[0]
            dst[2 * s + 1] = w[1]
            dst[C + 2 * s] = v[0]
            dst[C + 2 * s + 1] = v[1]

    def fwd_copy(j, k, source):
        return remote(
            fwd_send.at[j, k], gathered.at[source, k], fwd_s.at[j, k], fwd_r.at[source, k],
            place_of(j),
        )

    others = [fellow(step) for step in range(1, M)]

    def give(k, carry):
        for j in others:
            local(j, k, fwd_send.at[j, k])
        for j in others:
            fwd_copy(j, k, m).start()
        return carry

    def keep(k, carry):
        local(m, k, gathered.at[m, k])
        return carry

    lax.fori_loop(0, K, give, 0)
    lax.fori_loop(0, K, keep, 0)

    pad = comb.shape[1] // 2 - X // 2
    column = jnp.where(py == 0, Y - 1, 0)
    chunk_lane = lax.broadcasted_iota(jnp.int32, (R, LANES), 1)

    def full(half, k):
        row = half * H + k * R
        at = pl.ds(pl.multiple_of(row, R), R)
        to = pl.ds(pl.multiple_of(row + pad, 8), R)
        rates = [(rate_re[l, at], rate_im[l, at]) for l in range(L)]
        held = jnp.zeros((R, LANES), F32)
        for s in range(shots):
            i, j = 2 * s, 2 * s + 1
            f = [(force[l, i, at], force[l, j, at]) for l in range(L)]
            w = (enter_down[half, k, i], enter_down[half, k, j])
            downs = []
            for l in range(L):
                re, im = times(rates[l], w)
                w = (re + f[l][0], im + f[l][1])
                downs.append(w)
            v = (enter_up[half, k, i], enter_up[half, k, j])
            for l in range(L - 1, -1, -1):
                turn = times(rates[l], v)
                for a in (0, 1):
                    plane = l * C + i + a
                    value = downs[l][a] + turn[a]
                    comb[plane, to] = value
                    shift = lax.rem(plane + LANES - column, LANES)
                    held = jnp.where(chunk_lane == plane, pltpu.roll(value, shift, 1), held)
                v = (turn[0] + f[l][0], turn[1] + f[l][1])
        col_send[at] = held

    @pl.when(g == 0)
    def _():
        down_recv[...] = jnp.zeros_like(down_recv)

    @pl.when(g == G - 1)
    def _():
        up_recv[...] = jnp.zeros_like(up_recv)

    def down_copy(k, to):
        return remote(down_send.at[k], down_recv.at[k], down_s.at[k], down_r.at[k], {"slab": to})

    def up_copy(k, to):
        return remote(up_send.at[k], up_recv.at[k], up_s.at[k], up_r.at[k], {"slab": to})

    def down_back_copy(j, k, source):
        return remote(
            down_back.at[j, k], enter_down.at[source, k], dback_s.at[j, k], dback_r.at[source, k],
            place_of(j),
        )

    def up_back_copy(j, k, source):
        return remote(
            up_back.at[j, k], enter_up.at[source, k], uback_s.at[j, k], uback_r.at[source, k],
            place_of(j),
        )

    def hop(k, order, base, incoming, outgoing, back, own):
        at = pl.ds(pl.multiple_of(k * R, R), R)
        for s in range(shots):
            i, j = 2 * s, 2 * s + 1
            e = (incoming[k, i], incoming[k, j])
            for member in order:
                back[member, k, i] = e[0]
                back[member, k, j] = e[1]
                re, im = times((prod_all[member, 0, at], prod_all[member, 1, at]), e)
                e = (re + gathered[member, k, base + i], im + gathered[member, k, base + j])
            outgoing[k, i] = e[0]
            outgoing[k, j] = e[1]
        own[m, k] = back[m, k]

    def take_products(step, carry):
        j = fellow(step)
        prod_copy(j, j).wait_recv()
        return carry

    lax.fori_loop(1, M, take_products, 0)
    ready = jnp.maximum(g, G - 1 - g)

    def chain(t, carry):
        @pl.when(t < K)
        def _():
            for step in range(1, M):
                j = fellow(step)
                fwd_copy(j, t, j).wait_recv()

        kd = t - g
        ku = t - (G - 1 - g)
        has_down = (kd >= 0) & (kd < K)
        has_up = (ku >= 0) & (ku < K)

        @pl.when(has_down)
        def _():
            @pl.when(g > 0)
            def _():
                down_copy(kd, me - M).wait_recv()

            hop(kd, range(M), 0, down_recv, down_send, down_back, enter_down)

            @pl.when(g < G - 1)
            def _():
                down_copy(kd, me + M).start()

            for step in range(1, M):
                down_back_copy(fellow(step), kd, m).start()

        @pl.when(has_up)
        def _():
            @pl.when(g < G - 1)
            def _():
                up_copy(ku, me + M).wait_recv()

            hop(ku, range(M - 1, -1, -1), C, up_recv, up_send, up_back, enter_up)

            @pl.when(g > 0)
            def _():
                up_copy(ku, me - M).start()

            for step in range(1, M):
                up_back_copy(fellow(step), ku, m).start()

        ke = t - ready

        @pl.when((ke >= 0) & (ke < K))
        def _():
            full(m, ke)

        return carry

    lax.fori_loop(0, K + G - 1, chain, 0)

    def finish(k, carry):
        for j in others:
            down_back_copy(j, k, j).wait_recv()
            up_back_copy(j, k, j).wait_recv()
        for j in others:
            full(j, k)
        return carry

    lax.fori_loop(0, K, finish, 0)

    cols_out = remote(col_send, col_recv, col_s, col_r, other_y)
    cols_out.start()
    planes = L * C

    def send_rows(row):
        for i in range(planes):
            row_send[i : i + 1, :] = comb[i, pad + row : pad + row + 1, :]

    pl.when(px == 0)(lambda: send_rows(X - 1))
    pl.when(px == 1)(lambda: send_rows(0))
    rows_out = remote(row_send, row_recv, row_s, row_r, other_x)
    rows_out.start()

    full_lane = lax.broadcasted_iota(jnp.int32, (X, Y), 1)

    def stencil(i, carry):
        comb[i, pad - 1 : pad, :] = jnp.zeros((1, Y), F32)
        comb[i, pad + X : pad + X + 1, :] = jnp.zeros((1, Y), F32)
        here = comb[i, pad : pad + X, :]
        around = comb[i, pad - 1 : pad - 1 + X, :] + comb[i, pad + 1 : pad + 1 + X, :]
        around += jnp.where(full_lane == 0, 0.0, pltpu.roll(here, 1, 1))
        around += jnp.where(full_lane == Y - 1, 0.0, pltpu.roll(here, Y - 1, 1))
        out[lax.div(i, C), lax.rem(i, C)] = here - 0.2 * (4.0 * here - around)
        return carry

    lax.fori_loop(0, planes, stencil, 0)
    cols_out.wait_recv()
    at_edge = full_lane == column

    def add_columns(i, carry):
        shift = lax.rem(column + LANES - i, LANES)
        moved = pltpu.roll(col_recv[...], shift, 1)
        out[lax.div(i, C), lax.rem(i, C)] += jnp.where(at_edge, 0.2 * moved, 0.0)
        return carry

    lax.fori_loop(0, planes, add_columns, 0)
    rows_out.wait_recv()

    def add_rows(row):
        for l in range(L):
            for c in range(C):
                out[l, c, row : row + 1, :] += 0.2 * row_recv[l * C + c : l * C + c + 1, :]

    pl.when(px == 0)(lambda: add_rows(X - 1))
    pl.when(px == 1)(lambda: add_rows(0))

    for copy in spreads + [rows_out, cols_out]:
        copy.wait_send()

    def drain(step, carry):
        j = fellow(step)
        prod_copy(j, m).wait_send()
        for k in range(K):
            fwd_copy(j, k, m).wait_send()
            down_back_copy(j, k, m).wait_send()
            up_back_copy(j, k, m).wait_send()
        return carry

    lax.fori_loop(1, M, drain, 0)

    @pl.when(g < G - 1)
    def _():
        for k in range(K):
            down_copy(k, me + M).wait_send()

    @pl.when(g > 0)
    def _():
        for k in range(K):
            up_copy(k, me - M).wait_send()


def shards(source, phase, attenuation, pml_level, recv_values, recv_slab, recv_lateral, recv_layer):
    L, C, X, Y = source.shape
    S = lax.axis_size("slab")
    rows = recv_values.shape[3]
    K, M = CHUNKS, GROUP
    H = X // M
    R = H // K
    vmem, dma = pltpu.VMEM, pltpu.SemaphoreType.DMA
    chunked = vmem((K, C, R, Y), F32)
    spaced = vmem((M, K, C, R, Y), F32)
    scratch = [
        vmem((C, rows), F32), vmem((1, rows), jnp.int32), vmem((1, rows), jnp.int32), vmem((1, rows), jnp.int32),
        vmem((L, C, X, Y), F32), vmem((L, X, Y), F32), vmem((L, X, Y), F32), vmem((X, Y), jnp.int32),
        vmem((L, X, Y), F32), vmem((L, X, Y), F32),
        vmem((8, rows), F32), vmem((S // 2, 8, LANES), F32), vmem((S, 8, LANES), F32),
        vmem((L * X, S * CAP), BF16), vmem((C * Y, 3 * S * CAP), BF16),
        vmem((M, 2, H, Y), F32), vmem((M, 2, H, Y), F32),
        vmem((M, K, 2 * C, R, Y), F32), vmem((M, K, 2 * C, R, Y), F32),
        chunked, chunked, chunked, chunked, spaced, spaced, spaced, spaced,
        vmem((L * C, X + 16, Y), F32),
        vmem((L * C, Y), F32), vmem((L * C, Y), F32), vmem((X, LANES), F32), vmem((X, LANES), F32),
        dma((8,)), dma((S,)), dma((S,)), dma((M,)), dma((M,)), dma((M, K)), dma((M, K)),
        dma((K,)), dma((K,)), dma((K,)), dma((K,)),
        dma((M, K)), dma((M, K)), dma((M, K)), dma((M, K)),
        dma, dma, dma, dma,
    ]
    in_hbm = pl.BlockSpec(memory_space=pltpu.HBM)
    in_vmem = pl.BlockSpec(memory_space=pltpu.VMEM)
    return pl.pallas_call(
        functools.partial(kernel, (S, L, C, X, Y, K, M)),
        out_shape=jax.ShapeDtypeStruct(source.shape, F32),
        in_specs=[in_hbm] * 8,
        out_specs=in_vmem,
        scratch_shapes=scratch,
        compiler_params=pltpu.CompilerParams(
            collective_id=0, has_side_effects=True, vmem_limit_bytes=VMEM_BYTES
        ),
    )(*(
        pltpu.with_memory_space_constraint(x, pltpu.HBM)
        for x in (
            source, phase, attenuation, pml_level,
            recv_values[0, 0], recv_slab.reshape(1, rows), recv_lateral[0], recv_layer[0],
        )
    ))


def solution(mesh):
    in_specs = (
        P("slab", None, "px", "py"),
        P("slab", "px", "py"),
        P("slab", "px", "py"),
        P("px", "py"),
        P("px", "py", None, "slab"),
        P("px", "py", "slab", None),
        P("px", "py", "slab"),
        P("px", "py", "slab"),
    )
    out_specs = P("slab", None, "px", "py")
    return jax.shard_map(shards, mesh=mesh, in_specs=in_specs, out_specs=out_specs, check_vma=False)
```

```python
import functools

import jax
import jax.numpy as jnp
from jax import lax
from jax.experimental import pallas as pl
from jax.experimental.pallas import tpu as pltpu
from jax.sharding import PartitionSpec as P

GROUP = 4
CHUNKS = 1
LANES = 128
CAP = 64
VMEM_BYTES = 48 * 1024 * 1024
BF16 = jnp.bfloat16
F32 = jnp.float32


def thirds(value):
    high = value.astype(BF16)
    rest = value - high.astype(F32)
    mid = rest.astype(BF16)
    low = (rest - mid.astype(F32)).astype(BF16)
    return high, mid, low


def times(rate, state):
    return rate[0] * state[0] - rate[1] * state[1], rate[0] * state[1] + rate[1] * state[0]


def circle(angle):
    t = (angle - 1.5707963705062866) + 4.371139000186241e-08
    z = t * t
    odd = -1.0 / 39916800.0
    for factor in (1.0 / 362880.0, -1.0 / 5040.0, 1.0 / 120.0, -1.0 / 6.0):
        odd = odd * z + factor
    even = 1.0 / 479001600.0
    for factor in (-1.0 / 3628800.0, 1.0 / 40320.0, -1.0 / 720.0, 1.0 / 24.0, -0.5):
        even = even * z + factor
    return -(t + t * z * odd), 1.0 + z * even


def kernel(
    sizes,
    src_hbm, phase_hbm, att_hbm, pml_hbm, vals_hbm, slab_hbm, lat_hbm, lay_hbm,
    out,
    vals, rslab, rlat, rlay, force, phase, att, pml, rate_re, rate_im,
    data, spread, arrived, left, right,
    prod_send, prod_all, fwd_send, gathered,
    down_send, down_recv, up_send, up_recv,
    down_back, up_back, enter_down, enter_up,
    comb, row_send, row_recv, col_send, col_recv,
    in_sem, spread_s, spread_r, prod_s, prod_r, fwd_s, fwd_r,
    down_s, down_r, up_s, up_r, dback_s, dback_r, uback_s, uback_r,
    row_s, row_r, col_s, col_r,
):
    S, L, C, X, Y, K, M = sizes
    G = S // M
    H = X // M
    R = H // K
    shots = C // 2
    me = lax.axis_index("slab")
    px = lax.axis_index("px")
    py = lax.axis_index("py")
    g = lax.div(me, M)
    m = lax.rem(me, M)
    fellows = M - 1
    other_x = {"px": 1 - px}
    other_y = {"py": 1 - py}

    def fellow(step):
        return lax.rem(m + step, M)

    def place_of(member):
        return {"slab": g * M + member}

    def remote(src, dst, send, recv, where):
        return pltpu.make_async_remote_copy(
            src_ref=src, dst_ref=dst, send_sem=send, recv_sem=recv,
            device_id=where, device_id_type=pl.DeviceIdType.MESH,
        )

    barrier = pltpu.get_barrier_semaphore()
    peers = [lax.rem(me + step, S) for step in range(1, S)]
    for where in [{"slab": peer} for peer in peers] + [other_x, other_y]:
        pl.semaphore_signal(barrier, inc=1, device_id=where, device_id_type=pl.DeviceIdType.MESH)

    loads = [
        pltpu.make_async_copy(a, b, in_sem.at[i])
        for i, (a, b) in enumerate(
            (
                (slab_hbm, rslab), (vals_hbm, vals), (lat_hbm, rlat), (lay_hbm, rlay),
                (phase_hbm, phase), (att_hbm, att), (pml_hbm, pml), (src_hbm, force),
            )
        )
    ]
    for load in loads:
        load.start()

    for load in loads[:4]:
        load.wait()
    rows = vals.shape[1]
    blocks = rows // LANES
    slab_of = rslab[...]
    hot = jnp.where(lax.broadcasted_iota(jnp.int32, (S, rows), 0) == slab_of, 1.0, 0.0)
    cuts = [hot[:, i * LANES : (i + 1) * LANES] for i in range(blocks)]
    earlier = jnp.where(
        lax.broadcasted_iota(jnp.int32, (LANES, LANES), 0)
        < lax.broadcasted_iota(jnp.int32, (LANES, LANES), 1),
        1.0, 0.0,
    ).astype(BF16)
    within = jnp.dot(
        jnp.concatenate(cuts, axis=0).astype(BF16), earlier, preferred_element_type=F32
    )
    passed = jnp.zeros((S, 1), F32)
    ranks = []
    for i in range(blocks):
        ranks.append(
            jnp.sum((within[i * S : (i + 1) * S] + passed) * cuts[i], axis=0, keepdims=True)
        )
        passed = passed + jnp.sum(cuts[i], axis=1, keepdims=True)
    slot = slab_of * CAP + jnp.concatenate(ranks, axis=1).astype(jnp.int32)
    lateral = rlat[...]
    data[...] = jnp.zeros_like(data)
    data[0:C, :] = vals[...]
    data[C : C + 1, :] = (rlay[...] * X + lax.div(lateral, Y)).astype(F32)
    data[C + 1 : C + 2, :] = lax.rem(lateral, Y).astype(F32)
    pieces = jnp.concatenate([part.astype(F32) for part in thirds(data[...])], axis=0).astype(BF16)
    slot_at = lax.broadcasted_iota(jnp.int32, (LANES, rows), 0)

    def route(s, carry):
        place = jnp.where(slot_at + s * LANES == slot, 1.0, 0.0).astype(BF16)
        routed = lax.dot_general(
            pieces, place, (((1,), (1,)), ((), ())), preferred_element_type=F32
        )
        spread[s] = routed[0:8] + routed[8:16] + routed[16:24]
        return carry

    lax.fori_loop(0, S // 2, route, 0, unroll=4)

    pl.semaphore_wait(barrier, S + 1)
    arrived[me] = spread[lax.div(me, 2)]
    spreads = []
    for peer in peers:
        copy = remote(
            spread.at[lax.div(peer, 2)], arrived.at[me], spread_s.at[peer], spread_r.at[me], {"slab": peer}
        )
        copy.start()
        spreads.append(copy)

    for load in loads[4:7]:
        load.wait()

    def rate(l, carry):
        damping = att[l] + (0.5 / (L * S)) * pml[...].astype(F32)
        amplitude = jnp.exp(-damping)
        cosine, sine = circle(phase[l])
        rate_re[l] = amplitude * cosine
        rate_im[l] = amplitude * sine
        return carry

    lax.fori_loop(0, L, rate, 0)

    def product(half):
        at = pl.ds(pl.multiple_of(half * H, H), H)
        total = (rate_re[0, at], rate_im[0, at])
        for l in range(1, L):
            total = times((rate_re[l, at], rate_im[l, at]), total)
        return total

    def prod_copy(j, source):
        return remote(
            prod_send.at[j], prod_all.at[source], prod_s.at[j], prod_r.at[source], place_of(j)
        )

    def give_product(step, carry):
        j = fellow(step)
        total = product(j)
        prod_send[j, 0] = total[0]
        prod_send[j, 1] = total[1]
        prod_copy(j, m).start()
        return carry

    lax.fori_loop(1, M, give_product, 0)
    total = product(m)
    prod_all[m, 0] = total[0]
    prod_all[m, 1] = total[1]

    for peer in peers:
        remote(
            spread.at[lax.div(peer, 2)], arrived.at[peer], spread_s.at[peer], spread_r.at[peer], {"slab": peer}
        ).wait_recv()
    slots = S * CAP
    low_half = lax.broadcasted_iota(jnp.int32, (8, LANES), 1) < CAP
    keeps_low = lax.rem(me, 2) == 0

    def packed(i):
        a, b = arrived[2 * i], arrived[2 * i + 1]
        low = jnp.where(keeps_low, a, pltpu.roll(a, CAP, 1))
        high = jnp.where(keeps_low, pltpu.roll(b, CAP, 1), b)
        return jnp.where(low_half, low, high)

    got = jnp.concatenate([packed(i) for i in range(S // 2)], axis=1)
    row_at = got[C : C + 1, :].astype(jnp.int32)
    col_at = got[C + 1 : C + 2, :].astype(jnp.int32)
    left[...] = jnp.where(
        lax.broadcasted_iota(jnp.int32, (L * X, slots), 0) == row_at, 1.0, 0.0
    ).astype(BF16)
    on_col = lax.broadcasted_iota(jnp.int32, (Y, slots), 0) == col_at
    parts = [part.astype(F32) for part in thirds(got)]
    loads[7].wait()
    for s in range(shots):
        for i in range(3):
            for a in (0, 1):
                c = 2 * s + a
                right[c * Y : (c + 1) * Y, i * slots : (i + 1) * slots] = jnp.where(
                    on_col, parts[i][c : c + 1, :], 0.0
                ).astype(BF16)
        added = lax.dot_general(
            jnp.concatenate([left[...]] * 3, axis=1), right[2 * s * Y : (2 * s + 2) * Y, :],
            (((1,), (1,)), ((), ())), preferred_element_type=F32,
        )
        for l in range(L):
            for a in (0, 1):
                force[l, 2 * s + a] += added[l * X : (l + 1) * X, a * Y : (a + 1) * Y]

    def local(half, k, dst):
        at = pl.ds(pl.multiple_of(half * H + k * R, R), R)
        rates = [(rate_re[l, at], rate_im[l, at]) for l in range(L)]
        for s in range(shots):
            f = [(force[l, 2 * s, at], force[l, 2 * s + 1, at]) for l in range(L)]
            w = f[0]
            for l in range(1, L):
                re, im = times(rates[l], w)
                w = (re + f[l][0], im + f[l][1])
            v = f[L - 1]
            for l in range(L - 2, -1, -1):
                re, im = times(rates[l], v)
                v = (re + f[l][0], im + f[l][1])
            dst[2 * s] = w[0]
            dst[2 * s + 1] = w[1]
            dst[C + 2 * s] = v[0]
            dst[C + 2 * s + 1] = v[1]

    def fwd_copy(j, k, source):
        return remote(
            fwd_send.at[j, k], gathered.at[source, k], fwd_s.at[j, k], fwd_r.at[source, k],
            place_of(j),
        )

    def give(i, carry):
        k, j = lax.div(i, fellows), fellow(1 + lax.rem(i, fellows))
        local(j, k, fwd_send.at[j, k])
        fwd_copy(j, k, m).start()
        return carry

    def keep(k, carry):
        local(m, k, gathered.at[m, k])
        return carry

    lax.fori_loop(0, K * fellows, give, 0)
    lax.fori_loop(0, K, keep, 0)

    pad = comb.shape[1] // 2 - X // 2
    column = jnp.where(py == 0, Y - 1, 0)
    chunk_lane = lax.broadcasted_iota(jnp.int32, (R, LANES), 1)

    def full(half, k):
        row = half * H + k * R
        at = pl.ds(pl.multiple_of(row, R), R)
        to = pl.ds(pl.multiple_of(row + pad, 8), R)
        rates = [(rate_re[l, at], rate_im[l, at]) for l in range(L)]
        held = jnp.zeros((R, LANES), F32)
        for s in range(shots):
            i, j = 2 * s, 2 * s + 1
            f = [(force[l, i, at], force[l, j, at]) for l in range(L)]
            w = (enter_down[half, k, i], enter_down[half, k, j])
            downs = []
            for l in range(L):
                re, im = times(rates[l], w)
                w = (re + f[l][0], im + f[l][1])
                downs.append(w)
            v = (enter_up[half, k, i], enter_up[half, k, j])
            for l in range(L - 1, -1, -1):
                turn = times(rates[l], v)
                for a in (0, 1):
                    plane = l * C + i + a
                    value = downs[l][a] + turn[a]
                    comb[plane, to] = value
                    shift = lax.rem(plane + LANES - column, LANES)
                    held = jnp.where(chunk_lane == plane, pltpu.roll(value, shift, 1), held)
                v = (turn[0] + f[l][0], turn[1] + f[l][1])
        col_send[at] = held

    @pl.when(g == 0)
    def _():
        down_recv[...] = jnp.zeros_like(down_recv)

    @pl.when(g == G - 1)
    def _():
        up_recv[...] = jnp.zeros_like(up_recv)

    def down_copy(k, to):
        return remote(down_send.at[k], down_recv.at[k], down_s.at[k], down_r.at[k], {"slab": to})

    def up_copy(k, to):
        return remote(up_send.at[k], up_recv.at[k], up_s.at[k], up_r.at[k], {"slab": to})

    def down_back_copy(j, k, source):
        return remote(
            down_back.at[j, k], enter_down.at[source, k], dback_s.at[j, k], dback_r.at[source, k],
            place_of(j),
        )

    def up_back_copy(j, k, source):
        return remote(
            up_back.at[j, k], enter_up.at[source, k], uback_s.at[j, k], uback_r.at[source, k],
            place_of(j),
        )

    def hop(k, order, base, incoming, outgoing, back, own):
        at = pl.ds(pl.multiple_of(k * R, R), R)
        for s in range(shots):
            i, j = 2 * s, 2 * s + 1
            e = (incoming[k, i], incoming[k, j])
            for member in order:
                back[member, k, i] = e[0]
                back[member, k, j] = e[1]
                re, im = times((prod_all[member, 0, at], prod_all[member, 1, at]), e)
                e = (re + gathered[member, k, base + i], im + gathered[member, k, base + j])
            outgoing[k, i] = e[0]
            outgoing[k, j] = e[1]
        own[m, k] = back[m, k]

    def take_products(step, carry):
        j = fellow(step)
        prod_copy(j, j).wait_recv()
        return carry

    lax.fori_loop(1, M, take_products, 0)
    ready = jnp.maximum(g, G - 1 - g)

    def chain(t, carry):
        @pl.when(t < K)
        def _():
            for step in range(1, M):
                j = fellow(step)
                fwd_copy(j, t, j).wait_recv()

        kd = t - g
        ku = t - (G - 1 - g)
        has_down = (kd >= 0) & (kd < K)
        has_up = (ku >= 0) & (ku < K)

        @pl.when(has_down)
        def _():
            @pl.when(g > 0)
            def _():
                down_copy(kd, me - M).wait_recv()

            hop(kd, range(M), 0, down_recv, down_send, down_back, enter_down)

            @pl.when(g < G - 1)
            def _():
                down_copy(kd, me + M).start()

            for step in range(1, M):
                down_back_copy(fellow(step), kd, m).start()

        @pl.when(has_up)
        def _():
            @pl.when(g < G - 1)
            def _():
                up_copy(ku, me + M).wait_recv()

            hop(ku, range(M - 1, -1, -1), C, up_recv, up_send, up_back, enter_up)

            @pl.when(g > 0)
            def _():
                up_copy(ku, me - M).start()

            for step in range(1, M):
                up_back_copy(fellow(step), ku, m).start()

        ke = t - ready

        @pl.when((ke >= 0) & (ke < K))
        def _():
            full(m, ke)

        return carry

    lax.fori_loop(0, K + G - 1, chain, 0)

    def finish(i, carry):
        k, j = lax.div(i, fellows), fellow(1 + lax.rem(i, fellows))
        down_back_copy(j, k, j).wait_recv()
        up_back_copy(j, k, j).wait_recv()
        full(j, k)
        return carry

    lax.fori_loop(0, K * fellows, finish, 0)

    cols_out = remote(col_send, col_recv, col_s, col_r, other_y)
    cols_out.start()
    planes = L * C

    def send_rows(row):
        for i in range(planes):
            row_send[i : i + 1, :] = comb[i, pad + row : pad + row + 1, :]

    pl.when(px == 0)(lambda: send_rows(X - 1))
    pl.when(px == 1)(lambda: send_rows(0))
    rows_out = remote(row_send, row_recv, row_s, row_r, other_x)
    rows_out.start()

    full_lane = lax.broadcasted_iota(jnp.int32, (X, Y), 1)

    def stencil(i, carry):
        comb[i, pad - 1 : pad, :] = jnp.zeros((1, Y), F32)
        comb[i, pad + X : pad + X + 1, :] = jnp.zeros((1, Y), F32)
        here = comb[i, pad : pad + X, :]
        around = comb[i, pad - 1 : pad - 1 + X, :] + comb[i, pad + 1 : pad + 1 + X, :]
        around += jnp.where(full_lane == 0, 0.0, pltpu.roll(here, 1, 1))
        around += jnp.where(full_lane == Y - 1, 0.0, pltpu.roll(here, Y - 1, 1))
        out[lax.div(i, C), lax.rem(i, C)] = here - 0.2 * (4.0 * here - around)
        return carry

    lax.fori_loop(0, planes, stencil, 0)
    cols_out.wait_recv()
    at_edge = full_lane == column

    def add_columns(i, carry):
        shift = lax.rem(column + LANES - i, LANES)
        moved = pltpu.roll(col_recv[...], shift, 1)
        out[lax.div(i, C), lax.rem(i, C)] += jnp.where(at_edge, 0.2 * moved, 0.0)
        return carry

    lax.fori_loop(0, planes, add_columns, 0)
    rows_out.wait_recv()

    def add_rows(row):
        for l in range(L):
            for c in range(C):
                out[l, c, row : row + 1, :] += 0.2 * row_recv[l * C + c : l * C + c + 1, :]

    pl.when(px == 0)(lambda: add_rows(X - 1))
    pl.when(px == 1)(lambda: add_rows(0))

    for copy in spreads + [rows_out, cols_out]:
        copy.wait_send()

    def drain(step, carry):
        j = fellow(step)
        prod_copy(j, m).wait_send()
        for k in range(K):
            fwd_copy(j, k, m).wait_send()
            down_back_copy(j, k, m).wait_send()
            up_back_copy(j, k, m).wait_send()
        return carry

    lax.fori_loop(1, M, drain, 0)

    @pl.when(g < G - 1)
    def _():
        for k in range(K):
            down_copy(k, me + M).wait_send()

    @pl.when(g > 0)
    def _():
        for k in range(K):
            up_copy(k, me - M).wait_send()


def shards(source, phase, attenuation, pml_level, recv_values, recv_slab, recv_lateral, recv_layer):
    L, C, X, Y = source.shape
    S = lax.axis_size("slab")
    rows = recv_values.shape[3]
    K, M = CHUNKS, GROUP
    H = X // M
    R = H // K
    vmem, dma = pltpu.VMEM, pltpu.SemaphoreType.DMA
    chunked = vmem((K, C, R, Y), F32)
    spaced = vmem((M, K, C, R, Y), F32)
    scratch = [
        vmem((C, rows), F32), vmem((1, rows), jnp.int32), vmem((1, rows), jnp.int32), vmem((1, rows), jnp.int32),
        vmem((L, C, X, Y), F32), vmem((L, X, Y), F32), vmem((L, X, Y), F32), vmem((X, Y), jnp.int32),
        vmem((L, X, Y), F32), vmem((L, X, Y), F32),
        vmem((8, rows), F32), vmem((S // 2, 8, LANES), F32), vmem((S, 8, LANES), F32),
        vmem((L * X, S * CAP), BF16), vmem((C * Y, 3 * S * CAP), BF16),
        vmem((M, 2, H, Y), F32), vmem((M, 2, H, Y), F32),
        vmem((M, K, 2 * C, R, Y), F32), vmem((M, K, 2 * C, R, Y), F32),
        chunked, chunked, chunked, chunked, spaced, spaced, spaced, spaced,
        vmem((L * C, X + 16, Y), F32),
        vmem((L * C, Y), F32), vmem((L * C, Y), F32), vmem((X, LANES), F32), vmem((X, LANES), F32),
        dma((8,)), dma((S,)), dma((S,)), dma((M,)), dma((M,)), dma((M, K)), dma((M, K)),
        dma((K,)), dma((K,)), dma((K,)), dma((K,)),
        dma((M, K)), dma((M, K)), dma((M, K)), dma((M, K)),
        dma, dma, dma, dma,
    ]
    in_hbm = pl.BlockSpec(memory_space=pltpu.HBM)
    in_vmem = pl.BlockSpec(memory_space=pltpu.VMEM)
    return pl.pallas_call(
        functools.partial(kernel, (S, L, C, X, Y, K, M)),
        out_shape=jax.ShapeDtypeStruct(source.shape, F32),
        in_specs=[in_hbm] * 8,
        out_specs=in_vmem,
        scratch_shapes=scratch,
        compiler_params=pltpu.CompilerParams(
            collective_id=0, has_side_effects=True, vmem_limit_bytes=VMEM_BYTES
        ),
    )(*(
        pltpu.with_memory_space_constraint(x, pltpu.HBM)
        for x in (
            source, phase, attenuation, pml_level,
            recv_values[0, 0], recv_slab.reshape(1, rows), recv_lateral[0], recv_layer[0],
        )
    ))


def solution(mesh):
    in_specs = (
        P("slab", None, "px", "py"),
        P("slab", "px", "py"),
        P("slab", "px", "py"),
        P("px", "py"),
        P("px", "py", None, "slab"),
        P("px", "py", "slab", None),
        P("px", "py", "slab"),
        P("px", "py", "slab"),
    )
    out_specs = P("slab", None, "px", "py")
    return jax.shard_map(shards, mesh=mesh, in_specs=in_specs, out_specs=out_specs, check_vma=False)
```

```python
import functools

import jax
import jax.numpy as jnp
from jax import lax
from jax.experimental import pallas as pl
from jax.experimental.pallas import tpu as pltpu
from jax.sharding import PartitionSpec as P

GROUP = 4
CHUNKS = 1
LANES = 128
CAP = 64
VMEM_BYTES = 48 * 1024 * 1024
BF16 = jnp.bfloat16
F32 = jnp.float32


def thirds(value):
    high = value.astype(BF16)
    rest = value - high.astype(F32)
    mid = rest.astype(BF16)
    low = (rest - mid.astype(F32)).astype(BF16)
    return high, mid, low


def times(rate, state):
    return rate[0] * state[0] - rate[1] * state[1], rate[0] * state[1] + rate[1] * state[0]


def circle(angle):
    t = (angle - 1.5707963705062866) + 4.371139000186241e-08
    z = t * t
    odd = -1.0 / 39916800.0
    for factor in (1.0 / 362880.0, -1.0 / 5040.0, 1.0 / 120.0, -1.0 / 6.0):
        odd = odd * z + factor
    even = 1.0 / 479001600.0
    for factor in (-1.0 / 3628800.0, 1.0 / 40320.0, -1.0 / 720.0, 1.0 / 24.0, -0.5):
        even = even * z + factor
    return -(t + t * z * odd), 1.0 + z * even


def kernel(
    sizes,
    src_hbm, phase_hbm, att_hbm, pml_hbm, vals_hbm, slab_hbm, lat_hbm, lay_hbm,
    out,
    vals, rslab, rlat, rlay, force, phase, att, pml, rate_re, rate_im,
    data, spread, arrived, left, right,
    prod_send, prod_all, fwd_send, gathered,
    down_send, down_recv, up_send, up_recv,
    down_back, up_back, enter_down, enter_up,
    comb, row_send, row_recv, col_send, col_recv,
    in_sem, spread_s, spread_r, prod_s, prod_r, fwd_s, fwd_r,
    down_s, down_r, up_s, up_r, dback_s, dback_r, uback_s, uback_r,
    row_s, row_r, col_s, col_r,
):
    S, L, C, X, Y, K, M = sizes
    G = S // M
    H = X // M
    R = H // K
    shots = C // 2
    me = lax.axis_index("slab")
    px = lax.axis_index("px")
    py = lax.axis_index("py")
    g = lax.div(me, M)
    m = lax.rem(me, M)
    fellows = M - 1
    other_x = {"px": 1 - px}
    other_y = {"py": 1 - py}

    def fellow(step):
        first = lax.rem(lax.div(m, 2) + step % 2, 2)
        second = lax.rem(lax.rem(m, 2) + (M - step) // 2, 2)
        return 2 * first + second

    def place_of(member):
        return {"slab": g * M + member}

    def remote(src, dst, send, recv, where):
        return pltpu.make_async_remote_copy(
            src_ref=src, dst_ref=dst, send_sem=send, recv_sem=recv,
            device_id=where, device_id_type=pl.DeviceIdType.MESH,
        )

    barrier = pltpu.get_barrier_semaphore()
    peers = [lax.rem(me + step, S) for step in range(1, S)]
    for where in [{"slab": peer} for peer in peers] + [other_x, other_y]:
        pl.semaphore_signal(barrier, inc=1, device_id=where, device_id_type=pl.DeviceIdType.MESH)

    loads = [
        pltpu.make_async_copy(a, b, in_sem.at[i])
        for i, (a, b) in enumerate(
            (
                (slab_hbm, rslab), (vals_hbm, vals), (lat_hbm, rlat), (lay_hbm, rlay),
                (phase_hbm, phase), (att_hbm, att), (pml_hbm, pml), (src_hbm, force),
            )
        )
    ]
    for load in loads:
        load.start()

    for load in loads[:4]:
        load.wait()
    rows = vals.shape[1]
    blocks = rows // LANES
    slab_of = rslab[...]
    hot = jnp.where(lax.broadcasted_iota(jnp.int32, (S, rows), 0) == slab_of, 1.0, 0.0)
    cuts = [hot[:, i * LANES : (i + 1) * LANES] for i in range(blocks)]
    earlier = jnp.where(
        lax.broadcasted_iota(jnp.int32, (LANES, LANES), 0)
        < lax.broadcasted_iota(jnp.int32, (LANES, LANES), 1),
        1.0, 0.0,
    ).astype(BF16)
    within = jnp.dot(
        jnp.concatenate(cuts, axis=0).astype(BF16), earlier, preferred_element_type=F32
    )
    passed = jnp.zeros((S, 1), F32)
    ranks = []
    for i in range(blocks):
        ranks.append(
            jnp.sum((within[i * S : (i + 1) * S] + passed) * cuts[i], axis=0, keepdims=True)
        )
        passed = passed + jnp.sum(cuts[i], axis=1, keepdims=True)
    slot = slab_of * CAP + jnp.concatenate(ranks, axis=1).astype(jnp.int32)
    lateral = rlat[...]
    data[...] = jnp.zeros_like(data)
    data[0:C, :] = vals[...]
    data[C : C + 1, :] = (rlay[...] * X + lax.div(lateral, Y)).astype(F32)
    data[C + 1 : C + 2, :] = lax.rem(lateral, Y).astype(F32)
    pieces = jnp.concatenate([part.astype(F32) for part in thirds(data[...])], axis=0).astype(BF16)
    slot_at = lax.broadcasted_iota(jnp.int32, (LANES, rows), 0)

    def route(s, carry):
        place = jnp.where(slot_at + s * LANES == slot, 1.0, 0.0).astype(BF16)
        routed = lax.dot_general(
            pieces, place, (((1,), (1,)), ((), ())), preferred_element_type=F32
        )
        spread[s] = routed[0:8] + routed[8:16] + routed[16:24]
        return carry

    lax.fori_loop(0, S // 2, route, 0, unroll=4)

    pl.semaphore_wait(barrier, S + 1)
    arrived[me] = spread[lax.div(me, 2)]
    spreads = []
    for peer in peers:
        copy = remote(
            spread.at[lax.div(peer, 2)], arrived.at[me], spread_s.at[peer], spread_r.at[me], {"slab": peer}
        )
        copy.start()
        spreads.append(copy)

    for load in loads[4:7]:
        load.wait()

    def rate(l, carry):
        damping = att[l] + (0.5 / (L * S)) * pml[...].astype(F32)
        amplitude = jnp.exp(-damping)
        cosine, sine = circle(phase[l])
        rate_re[l] = amplitude * cosine
        rate_im[l] = amplitude * sine
        return carry

    lax.fori_loop(0, L, rate, 0)

    def product(half):
        at = pl.ds(pl.multiple_of(half * H, H), H)
        total = (rate_re[0, at], rate_im[0, at])
        for l in range(1, L):
            total = times((rate_re[l, at], rate_im[l, at]), total)
        return total

    def prod_copy(j, source):
        return remote(
            prod_send.at[j], prod_all.at[source], prod_s.at[j], prod_r.at[source], place_of(j)
        )

    def give_product(step, carry):
        j = fellow(step)
        total = product(j)
        prod_send[j, 0] = total[0]
        prod_send[j, 1] = total[1]
        prod_copy(j, m).start()
        return carry

    lax.fori_loop(1, M, give_product, 0)
    total = product(m)
    prod_all[m, 0] = total[0]
    prod_all[m, 1] = total[1]

    for peer in peers:
        remote(
            spread.at[lax.div(peer, 2)], arrived.at[peer], spread_s.at[peer], spread_r.at[peer], {"slab": peer}
        ).wait_recv()
    slots = S * CAP
    low_half = lax.broadcasted_iota(jnp.int32, (8, LANES), 1) < CAP
    keeps_low = lax.rem(me, 2) == 0

    def packed(i):
        a, b = arrived[2 * i], arrived[2 * i + 1]
        low = jnp.where(keeps_low, a, pltpu.roll(a, CAP, 1))
        high = jnp.where(keeps_low, pltpu.roll(b, CAP, 1), b)
        return jnp.where(low_half, low, high)

    got = jnp.concatenate([packed(i) for i in range(S // 2)], axis=1)
    row_at = got[C : C + 1, :].astype(jnp.int32)
    col_at = got[C + 1 : C + 2, :].astype(jnp.int32)
    left[...] = jnp.where(
        lax.broadcasted_iota(jnp.int32, (L * X, slots), 0) == row_at, 1.0, 0.0
    ).astype(BF16)
    on_col = lax.broadcasted_iota(jnp.int32, (Y, slots), 0) == col_at
    parts = [part.astype(F32) for part in thirds(got)]
    loads[7].wait()
    for s in range(shots):
        for i in range(3):
            for a in (0, 1):
                c = 2 * s + a
                right[c * Y : (c + 1) * Y, i * slots : (i + 1) * slots] = jnp.where(
                    on_col, parts[i][c : c + 1, :], 0.0
                ).astype(BF16)
        added = lax.dot_general(
            jnp.concatenate([left[...]] * 3, axis=1), right[2 * s * Y : (2 * s + 2) * Y, :],
            (((1,), (1,)), ((), ())), preferred_element_type=F32,
        )
        for l in range(L):
            for a in (0, 1):
                force[l, 2 * s + a] += added[l * X : (l + 1) * X, a * Y : (a + 1) * Y]

    def local(half, k, dst):
        at = pl.ds(pl.multiple_of(half * H + k * R, R), R)
        rates = [(rate_re[l, at], rate_im[l, at]) for l in range(L)]
        for s in range(shots):
            f = [(force[l, 2 * s, at], force[l, 2 * s + 1, at]) for l in range(L)]
            w = f[0]
            for l in range(1, L):
                re, im = times(rates[l], w)
                w = (re + f[l][0], im + f[l][1])
            v = f[L - 1]
            for l in range(L - 2, -1, -1):
                re, im = times(rates[l], v)
                v = (re + f[l][0], im + f[l][1])
            dst[2 * s] = w[0]
            dst[2 * s + 1] = w[1]
            dst[C + 2 * s] = v[0]
            dst[C + 2 * s + 1] = v[1]

    def fwd_copy(j, k, source):
        return remote(
            fwd_send.at[j, k], gathered.at[source, k], fwd_s.at[j, k], fwd_r.at[source, k],
            place_of(j),
        )

    def give(i, carry):
        k, j = lax.div(i, fellows), fellow(1 + lax.rem(i, fellows))
        local(j, k, fwd_send.at[j, k])
        fwd_copy(j, k, m).start()
        return carry

    def keep(k, carry):
        local(m, k, gathered.at[m, k])
        return carry

    lax.fori_loop(0, K * fellows, give, 0)
    lax.fori_loop(0, K, keep, 0)

    pad = comb.shape[1] // 2 - X // 2
    column = jnp.where(py == 0, Y - 1, 0)
    chunk_lane = lax.broadcasted_iota(jnp.int32, (R, LANES), 1)

    def full(half, k):
        row = half * H + k * R
        at = pl.ds(pl.multiple_of(row, R), R)
        to = pl.ds(pl.multiple_of(row + pad, 8), R)
        rates = [(rate_re[l, at], rate_im[l, at]) for l in range(L)]
        held = jnp.zeros((R, LANES), F32)
        for s in range(shots):
            i, j = 2 * s, 2 * s + 1
            f = [(force[l, i, at], force[l, j, at]) for l in range(L)]
            w = (enter_down[half, k, i], enter_down[half, k, j])
            downs = []
            for l in range(L):
                re, im = times(rates[l], w)
                w = (re + f[l][0], im + f[l][1])
                downs.append(w)
            v = (enter_up[half, k, i], enter_up[half, k, j])
            for l in range(L - 1, -1, -1):
                turn = times(rates[l], v)
                for a in (0, 1):
                    plane = l * C + i + a
                    value = downs[l][a] + turn[a]
                    comb[plane, to] = value
                    shift = lax.rem(plane + LANES - column, LANES)
                    held = jnp.where(chunk_lane == plane, pltpu.roll(value, shift, 1), held)
                v = (turn[0] + f[l][0], turn[1] + f[l][1])
        col_send[at] = held

    @pl.when(g == 0)
    def _():
        down_recv[...] = jnp.zeros_like(down_recv)

    @pl.when(g == G - 1)
    def _():
        up_recv[...] = jnp.zeros_like(up_recv)

    def down_copy(k, to):
        return remote(down_send.at[k], down_recv.at[k], down_s.at[k], down_r.at[k], {"slab": to})

    def up_copy(k, to):
        return remote(up_send.at[k], up_recv.at[k], up_s.at[k], up_r.at[k], {"slab": to})

    def down_back_copy(j, k, source):
        return remote(
            down_back.at[j, k], enter_down.at[source, k], dback_s.at[j, k], dback_r.at[source, k],
            place_of(j),
        )

    def up_back_copy(j, k, source):
        return remote(
            up_back.at[j, k], enter_up.at[source, k], uback_s.at[j, k], uback_r.at[source, k],
            place_of(j),
        )

    def hop(k, order, base, incoming, outgoing, back, own):
        at = pl.ds(pl.multiple_of(k * R, R), R)
        for s in range(shots):
            i, j = 2 * s, 2 * s + 1
            e = (incoming[k, i], incoming[k, j])
            for member in order:
                back[member, k, i] = e[0]
                back[member, k, j] = e[1]
                re, im = times((prod_all[member, 0, at], prod_all[member, 1, at]), e)
                e = (re + gathered[member, k, base + i], im + gathered[member, k, base + j])
            outgoing[k, i] = e[0]
            outgoing[k, j] = e[1]
        own[m, k] = back[m, k]

    def take_products(step, carry):
        j = fellow(step)
        prod_copy(j, j).wait_recv()
        return carry

    lax.fori_loop(1, M, take_products, 0)
    ready = jnp.maximum(g, G - 1 - g)

    def chain(t, carry):
        @pl.when(t < K)
        def _():
            for step in range(1, M):
                j = fellow(step)
                fwd_copy(j, t, j).wait_recv()

        kd = t - g
        ku = t - (G - 1 - g)
        has_down = (kd >= 0) & (kd < K)
        has_up = (ku >= 0) & (ku < K)

        @pl.when(has_down)
        def _():
            @pl.when(g > 0)
            def _():
                down_copy(kd, me - M).wait_recv()

            hop(kd, range(M), 0, down_recv, down_send, down_back, enter_down)

            @pl.when(g < G - 1)
            def _():
                down_copy(kd, me + M).start()

            for step in range(1, M):
                down_back_copy(fellow(step), kd, m).start()

        @pl.when(has_up)
        def _():
            @pl.when(g < G - 1)
            def _():
                up_copy(ku, me + M).wait_recv()

            hop(ku, range(M - 1, -1, -1), C, up_recv, up_send, up_back, enter_up)

            @pl.when(g > 0)
            def _():
                up_copy(ku, me - M).start()

            for step in range(1, M):
                up_back_copy(fellow(step), ku, m).start()

        ke = t - ready

        @pl.when((ke >= 0) & (ke < K))
        def _():
            full(m, ke)

        return carry

    lax.fori_loop(0, K + G - 1, chain, 0)

    def finish(i, carry):
        k, j = lax.div(i, fellows), fellow(fellows - lax.rem(i, fellows))
        down_back_copy(j, k, j).wait_recv()
        up_back_copy(j, k, j).wait_recv()
        full(j, k)
        return carry

    lax.fori_loop(0, K * fellows, finish, 0)

    cols_out = remote(col_send, col_recv, col_s, col_r, other_y)
    cols_out.start()
    planes = L * C

    def send_rows(row):
        for i in range(planes):
            row_send[i : i + 1, :] = comb[i, pad + row : pad + row + 1, :]

    pl.when(px == 0)(lambda: send_rows(X - 1))
    pl.when(px == 1)(lambda: send_rows(0))
    rows_out = remote(row_send, row_recv, row_s, row_r, other_x)
    rows_out.start()

    full_lane = lax.broadcasted_iota(jnp.int32, (X, Y), 1)

    def stencil(i, carry):
        comb[i, pad - 1 : pad, :] = jnp.zeros((1, Y), F32)
        comb[i, pad + X : pad + X + 1, :] = jnp.zeros((1, Y), F32)
        here = comb[i, pad : pad + X, :]
        around = comb[i, pad - 1 : pad - 1 + X, :] + comb[i, pad + 1 : pad + 1 + X, :]
        around += jnp.where(full_lane == 0, 0.0, pltpu.roll(here, 1, 1))
        around += jnp.where(full_lane == Y - 1, 0.0, pltpu.roll(here, Y - 1, 1))
        out[lax.div(i, C), lax.rem(i, C)] = here - 0.2 * (4.0 * here - around)
        return carry

    lax.fori_loop(0, planes, stencil, 0)
    cols_out.wait_recv()
    at_edge = full_lane == column

    def add_columns(i, carry):
        shift = lax.rem(column + LANES - i, LANES)
        moved = pltpu.roll(col_recv[...], shift, 1)
        out[lax.div(i, C), lax.rem(i, C)] += jnp.where(at_edge, 0.2 * moved, 0.0)
        return carry

    lax.fori_loop(0, planes, add_columns, 0)
    rows_out.wait_recv()

    def add_rows(row):
        for l in range(L):
            for c in range(C):
                out[l, c, row : row + 1, :] += 0.2 * row_recv[l * C + c : l * C + c + 1, :]

    pl.when(px == 0)(lambda: add_rows(X - 1))
    pl.when(px == 1)(lambda: add_rows(0))

    for copy in spreads + [rows_out, cols_out]:
        copy.wait_send()

    def drain(step, carry):
        j = fellow(step)
        prod_copy(j, m).wait_send()
        for k in range(K):
            fwd_copy(j, k, m).wait_send()
            down_back_copy(j, k, m).wait_send()
            up_back_copy(j, k, m).wait_send()
        return carry

    lax.fori_loop(1, M, drain, 0)

    @pl.when(g < G - 1)
    def _():
        for k in range(K):
            down_copy(k, me + M).wait_send()

    @pl.when(g > 0)
    def _():
        for k in range(K):
            up_copy(k, me - M).wait_send()


def shards(source, phase, attenuation, pml_level, recv_values, recv_slab, recv_lateral, recv_layer):
    L, C, X, Y = source.shape
    S = lax.axis_size("slab")
    rows = recv_values.shape[3]
    K, M = CHUNKS, GROUP
    H = X // M
    R = H // K
    vmem, dma = pltpu.VMEM, pltpu.SemaphoreType.DMA
    chunked = vmem((K, C, R, Y), F32)
    spaced = vmem((M, K, C, R, Y), F32)
    scratch = [
        vmem((C, rows), F32), vmem((1, rows), jnp.int32), vmem((1, rows), jnp.int32), vmem((1, rows), jnp.int32),
        vmem((L, C, X, Y), F32), vmem((L, X, Y), F32), vmem((L, X, Y), F32), vmem((X, Y), jnp.int32),
        vmem((L, X, Y), F32), vmem((L, X, Y), F32),
        vmem((8, rows), F32), vmem((S // 2, 8, LANES), F32), vmem((S, 8, LANES), F32),
        vmem((L * X, S * CAP), BF16), vmem((C * Y, 3 * S * CAP), BF16),
        vmem((M, 2, H, Y), F32), vmem((M, 2, H, Y), F32),
        vmem((M, K, 2 * C, R, Y), F32), vmem((M, K, 2 * C, R, Y), F32),
        chunked, chunked, chunked, chunked, spaced, spaced, spaced, spaced,
        vmem((L * C, X + 16, Y), F32),
        vmem((L * C, Y), F32), vmem((L * C, Y), F32), vmem((X, LANES), F32), vmem((X, LANES), F32),
        dma((8,)), dma((S,)), dma((S,)), dma((M,)), dma((M,)), dma((M, K)), dma((M, K)),
        dma((K,)), dma((K,)), dma((K,)), dma((K,)),
        dma((M, K)), dma((M, K)), dma((M, K)), dma((M, K)),
        dma, dma, dma, dma,
    ]
    in_hbm = pl.BlockSpec(memory_space=pltpu.HBM)
    in_vmem = pl.BlockSpec(memory_space=pltpu.VMEM)
    return pl.pallas_call(
        functools.partial(kernel, (S, L, C, X, Y, K, M)),
        out_shape=jax.ShapeDtypeStruct(source.shape, F32),
        in_specs=[in_hbm] * 8,
        out_specs=in_vmem,
        scratch_shapes=scratch,
        compiler_params=pltpu.CompilerParams(
            collective_id=0, has_side_effects=True, vmem_limit_bytes=VMEM_BYTES
        ),
    )(*(
        pltpu.with_memory_space_constraint(x, pltpu.HBM)
        for x in (
            source, phase, attenuation, pml_level,
            recv_values[0, 0], recv_slab.reshape(1, rows), recv_lateral[0], recv_layer[0],
        )
    ))


def solution(mesh):
    in_specs = (
        P("slab", None, "px", "py"),
        P("slab", "px", "py"),
        P("slab", "px", "py"),
        P("px", "py"),
        P("px", "py", None, "slab"),
        P("px", "py", "slab", None),
        P("px", "py", "slab"),
        P("px", "py", "slab"),
    )
    out_specs = P("slab", None, "px", "py")
    return jax.shard_map(shards, mesh=mesh, in_specs=in_specs, out_specs=out_specs, check_vma=False)
```
